32 devices in a mesh: group: 16 (over z, y, core), tp: 2 (over x).
Axes of the slice: x: 2, y: 2, z: 4, core: 2. Of those that a mesh axis runs over, the one named last changes fastest.
Arguments:
- tokens: bfloat16 [4096, 1024], P(('group', 'tp')), may hold values from -6 to 6
- variate: int32 [4096], P('group'), may hold values from 0 to 3
- time_ids: int32 [4096], P('group'), may hold values from 0 to 63
- cache_var: int32 [8192], P('group'), may hold values from 0 to 3
- cache_len: int32 [16], P('group'), may hold values from 1 to 512, as said below
- linked: int32 [16], P('group'), may hold values from 0 to 1, as said below
- cache_kv: bfloat16 [2, 8192, 1024], P(None, 'group', 'tp'), as said below
- var_bias: float32 [2, 16], P(None, 'tp'), may hold values from -2 to 2
- w_qkv: bfloat16 [3, 1024, 1024], P(None, None, 'tp'), may hold values from -0.1875 to 0.1875
- w_out: bfloat16 [1024, 1024], P('tp'), may hold values from -0.75 to 0.75
- w_gate_up: bfloat16 [2, 1024, 4096], P(None, None, 'tp'), may hold values from -0.1875 to 0.1875
- w_down: bfloat16 [4096, 1024], P('tp'), may hold values from -0.09375 to 0.09375
Outputs:
- layer_out: bfloat16 [4096, 1024], P(('group', 'tp'))
The draws below stay inside these ranges and needn't reach their ends.
Inputs may be any that keep to these rules, and one draw needn't show every extreme that they name: Group g's cached prefix fills its first cache_len[g] slots; some group has all 512. linked[g] equals linked[g + 8]; groups 0 and 8 are linked, and some other pair is not. `cache_kv`: cached keys already rotated, and cached values.
All inputs are finite; a program needn't handle non-finite values.
Results may differ from the reference program's by a relative error of at most 0.023.
Values may be sent and summed in bfloat16 or wider, within the bound.
No kernel may reach another device: no remote copies, remote signals or barrier semaphores. Data moves between devices by JAX's collectives and lax.ppermute only.
A program may use at most 64 MiB of HBM per device.

```python
import jax
import jax.numpy as jnp
from jax import lax

D = 1024
H = 16
HD = 64
FF = 4096
TOK_GRP = 256
CACHE = 512
GROUPS = 16
TOKENS = 4096


def draw_cache_len(key, part):
    first_key, second_key, third_key = jax.random.split(key, 3)
    shift_by = jax.random.randint(first_key, (GROUPS,), 0, 4)
    top_value = jnp.right_shift(jnp.full((GROUPS,), CACHE, jnp.int32), shift_by)
    cut_value = jax.random.randint(second_key, (GROUPS,), 0, 1 << 20) % (top_value // 2 + 1)
    lengths = jnp.maximum(top_value - cut_value, 1)
    place_at = jax.random.randint(third_key, (), 0, GROUPS)
    return jnp.where(jnp.arange(GROUPS) == place_at, CACHE, lengths).astype(jnp.int32)


def draw_linked(key, part):
    first_key, second_key = jax.random.split(key, 2)
    half_count = GROUPS // 2
    flags = jax.random.randint(first_key, (half_count,), 0, 2)
    second_pos = 1 + jax.random.randint(second_key, (), 0, half_count - 1)
    positions = jnp.arange(half_count)
    flags = jnp.where(positions == 0, 1, jnp.where(positions == second_pos, 0, flags))
    return jnp.concatenate([flags, flags]).astype(jnp.int32)


def draw_cache_kv(key, part):
    base_draw = jax.random.normal(key, (2, GROUPS * CACHE, H * HD), jnp.float32)
    return base_draw.astype(jnp.bfloat16)


def place_ends(entries, rng, least, largest):
    spot = [jax.random.randint(jax.random.fold_in(rng, axis), (), 0, length) for axis, length in enumerate(entries.shape)]
    main_axis = entries.shape.index(max(entries.shape))
    beside = spot[:main_axis] + [(spot[main_axis] + 1) % entries.shape[main_axis]] + spot[main_axis + 1:]
    return entries.at[tuple(spot)].set(least).at[tuple(beside)].set(largest)


def steps_of(own_key, dims, cuts, low, high):
    def one(dim, shards_of):
        heights = jax.random.uniform(jax.random.fold_in(jax.random.fold_in(own_key, 6), dim), (shards_of,), jnp.float32, low / len(cuts), high / len(cuts))
        return jnp.repeat(jnp.exp(heights), dims[dim] // shards_of).reshape((-1,) + (1,) * (len(dims) - dim - 1))

    factor_of = one(*cuts[0])
    for cut in cuts[1:]:
        factor_of = factor_of * one(*cut)
    return factor_of


def scatter_about(own_key, extent, width, bound, shards=(), held_as=jnp.bfloat16):
    level = steps_of(own_key, extent, shards, -0.22, 0.18) if shards else 1.0
    result = jax.random.normal(own_key, extent, jnp.float32) * width * level
    return jnp.minimum(jnp.maximum(result, -bound), bound).astype(held_as)


def setup_inputs(seed: int = 0) -> dict:
    key_of = jax.random.split(jax.random.key(seed), 13)
    tokens = scatter_about(key_of[0], (TOKENS, D), 1.0, 6.0, ((0, 32),))
    variate = place_ends(jax.random.randint(key_of[1], (TOKENS,), 0, 4), jax.random.fold_in(key_of[1], 1), 0, 3).astype(jnp.int32)
    time_ids = place_ends(jax.random.randint(key_of[2], (TOKENS,), 0, TOK_GRP // 4), jax.random.fold_in(key_of[2], 1), 0, (TOK_GRP // 4) - 1).astype(jnp.int32)
    cache_var = place_ends(jax.random.randint(key_of[3], (GROUPS * CACHE,), 0, 4), jax.random.fold_in(key_of[3], 1), 0, 3).astype(jnp.int32)
    cache_len = draw_cache_len(jax.random.fold_in(key_of[12], 71), 0)
    linked = draw_linked(jax.random.fold_in(key_of[12], 71), 0)
    cache_kv = draw_cache_kv(jax.random.fold_in(key_of[12], 71), 0)
    var_bias = jnp.clip(jax.random.uniform(key_of[7], (2, H), jnp.float32, -2.0, 2.0) * steps_of(key_of[7], (2, H), ((1, 2),), -0.4, 0.0), -2.0, 2.0)
    w_qkv = scatter_about(key_of[8], (3, D, H * HD), D ** -0.5, 0.1875, ((2, 2),))
    w_out = scatter_about(key_of[9], (H * HD, D), HD ** -0.5, 0.75, ((0, 2),))
    w_gate_up = scatter_about(key_of[10], (2, D, FF), D ** -0.5, 0.1875, ((2, 2),))
    w_down = scatter_about(key_of[11], (FF, D), FF ** -0.5, 0.09375, ((0, 2),))
    return {"tokens": tokens, "variate": variate, "time_ids": time_ids, "cache_var": cache_var, "cache_len": cache_len, "linked": linked, "cache_kv": cache_kv, "var_bias": var_bias, "w_qkv": w_qkv, "w_out": w_out, "w_gate_up": w_gate_up, "w_down": w_down}


far_future = 1073741824
masked_score = -1e+30

def normed(row_block):
    values = row_block.astype(jnp.float32)
    return values * lax.rsqrt(lax.optimization_barrier(jnp.mean(values * values, axis=-1, keepdims=True)) + 1e-05)

def rotary(values, position, head_count):
    row_count = values.shape[0]
    shaped = values.reshape(row_count, head_count, -1)
    half_width = shaped.shape[-1] // 2
    frequency = 10000.0 ** (-jnp.arange(half_width, dtype=jnp.float32) / half_width)
    angles = position.astype(jnp.float32)[:, None] * frequency[None, :]
    cosine = jnp.cos(angles)[:, None, :]
    sine_part = jnp.sin(angles)[:, None, :]
    lower_half = shaped[..., :half_width]
    upper_half = shaped[..., half_width:]
    turned = jnp.concatenate([lower_half * cosine - upper_half * sine_part, upper_half * cosine + lower_half * sine_part], axis=-1)
    return turned.reshape(row_count, -1)

def reference(tokens, variate, time_ids, cache_var, cache_len, linked, cache_kv, var_bias, w_qkv, w_out, w_gate_up, w_down):
    head_count = var_bias.shape[1]
    normal_in = normed(tokens).astype(jnp.bfloat16)
    projected = jnp.stack([jnp.dot(normal_in, w_qkv[part_index], preferred_element_type=jnp.float32) for part_index in range(3)])
    queries = rotary(projected[0], time_ids, head_count).astype(jnp.bfloat16)
    new_keys = rotary(projected[1], time_ids, head_count).astype(jnp.bfloat16)
    new_vals = projected[2].astype(jnp.bfloat16)
    new_kv = jnp.stack([new_keys, new_vals])

    def key_set(group_id):
        cache_part = lax.dynamic_slice_in_dim(cache_kv, group_id * CACHE, CACHE, 1)
        new_part = lax.dynamic_slice_in_dim(new_kv, group_id * TOK_GRP, TOK_GRP, 1)
        slot_ids = jnp.arange(CACHE, dtype=jnp.int32)
        cache_time = jnp.where(slot_ids < cache_len[group_id], -1, far_future).astype(jnp.int32)
        new_time = lax.dynamic_slice_in_dim(time_ids, group_id * TOK_GRP, TOK_GRP, 0).astype(jnp.int32)
        key_time = jnp.concatenate([cache_time, new_time])
        key_var = jnp.concatenate([lax.dynamic_slice_in_dim(cache_var, group_id * CACHE, CACHE, 0).astype(jnp.int32), lax.dynamic_slice_in_dim(variate, group_id * TOK_GRP, TOK_GRP, 0).astype(jnp.int32)])
        return (jnp.concatenate([cache_part, new_part], axis=1), key_time, key_var)

    def one_group(group_id):
        partner_id = jnp.bitwise_xor(group_id, GROUPS // 2).astype(jnp.int32)
        own_kv, own_time, own_var = key_set(group_id)
        far_kv, far_time, far_var = key_set(partner_id)
        far_time = jnp.where(linked[group_id] > 0, far_time, far_future).astype(jnp.int32)
        key_vals = jnp.concatenate([own_kv, far_kv], axis=1)
        key_time = jnp.concatenate([own_time, far_time])
        key_var = jnp.concatenate([own_var, far_var])
        query_rows = lax.dynamic_slice_in_dim(queries, group_id * TOK_GRP, TOK_GRP, 0)
        query_time = lax.dynamic_slice_in_dim(time_ids, group_id * TOK_GRP, TOK_GRP, 0)
        query_var = lax.dynamic_slice_in_dim(variate, group_id * TOK_GRP, TOK_GRP, 0)
        query_heads = query_rows.reshape(TOK_GRP, head_count, -1).astype(jnp.float32)
        key_heads = key_vals[0].reshape(key_vals.shape[1], head_count, -1).astype(jnp.float32)
        value_heads = key_vals[1].reshape(key_vals.shape[1], head_count, -1).astype(jnp.float32)
        scores = jnp.einsum('thd,khd->htk', query_heads, key_heads) * 0.125
        same_variate = (query_var[:, None] == key_var[None, :])[None]
        scores = scores + jnp.where(same_variate, var_bias[0][:, None, None], var_bias[1][:, None, None])
        visible = (key_time[None, :] <= query_time[:, None])[None]
        scores = jnp.where(visible, scores, masked_score)
        row_best = lax.optimization_barrier(jnp.max(scores, axis=-1, keepdims=True))
        weights = jnp.exp(scores - row_best)
        denom = lax.optimization_barrier(jnp.sum(weights, axis=-1))
        rounded = lax.optimization_barrier(weights.astype(jnp.bfloat16)).astype(jnp.float32)
        attended = jnp.einsum('htk,khd->htd', rounded, value_heads) / denom[..., None]
        return attended.transpose(1, 0, 2).reshape(TOK_GRP, -1).astype(jnp.bfloat16)
    attn_heads = lax.map(one_group, jnp.arange(GROUPS, dtype=jnp.int32)).reshape(TOKENS, -1)
    stream = (tokens.astype(jnp.float32) + jnp.dot(attn_heads, w_out, preferred_element_type=jnp.float32)).astype(jnp.bfloat16)
    normed_mid = normed(stream).astype(jnp.bfloat16)
    gate_part = jnp.dot(normed_mid, w_gate_up[0], preferred_element_type=jnp.float32)
    up_part = jnp.dot(normed_mid, w_gate_up[1], preferred_element_type=jnp.float32)
    hidden = (jax.nn.silu(gate_part) * up_part).astype(jnp.bfloat16)
    ffn_out = jnp.dot(hidden, w_down, preferred_element_type=jnp.float32)
    return (stream.astype(jnp.float32) + ffn_out).astype(jnp.bfloat16)
```

```python
import functools
import math

import jax
import jax.numpy as jnp
from jax import lax
from jax.experimental import pallas as pl
from jax.experimental.pallas import tpu as pltpu
from jax.sharding import PartitionSpec as P

LANES = 128
HEAD = 64
STAT_ROWS = 16
LOG2E = math.log2(math.e)
MASKED = -1e30
F32 = jnp.float32
BF16 = jnp.bfloat16

IN_VMEM = pl.BlockSpec(memory_space=pltpu.VMEM)
IN_SMEM = pl.BlockSpec(memory_space=pltpu.SMEM)


def call(body, outs, *operands, scalars=(), flops=0, scratch=()):
    shapes = [jax.ShapeDtypeStruct(shape, dtype) for shape, dtype in outs]
    moved = sum(x.size * x.dtype.itemsize for x in operands)
    return pl.pallas_call(
        body,
        out_shape=shapes,
        in_specs=[IN_SMEM] * len(scalars) + [IN_VMEM] * len(operands),
        out_specs=[IN_VMEM] * len(shapes),
        scratch_shapes=list(scratch),
        cost_estimate=pl.CostEstimate(flops=flops, bytes_accessed=moved, transcendentals=0),
        compiler_params=pltpu.CompilerParams(vmem_limit_bytes=32 << 20),
    )(*scalars, *operands)


def swap(block, axis, distance):
    count = lax.axis_size(axis)
    return lax.ppermute(block, axis, [(i, i ^ distance) for i in range(count)])


def normed(values):
    return (values * lax.rsqrt(jnp.mean(values * values, axis=-1, keepdims=True) + 1e-05)).astype(
        BF16
    )


def iota(shape, dim):
    return lax.broadcasted_iota(jnp.int32, shape, dim)


def dot(a, b, contract=(1, 0)):
    return lax.dot_general(
        a, b, (((contract[0],), (contract[1],)), ((), ())), preferred_element_type=F32
    )


def three_parts(value):
    high = value.astype(BF16)
    rest = value - high.astype(F32)
    middle = rest.astype(BF16)
    low = (rest - middle.astype(F32)).astype(BF16)
    return high, middle, low


def first_chunk(by_owner):
    return lax.axis_index("tp") if by_owner else 0


def row_tables(time_row, var_row):
    sub = iota((LANES, LANES), 0)
    time_hot = jnp.where((sub & (HEAD - 1)) == time_row, 1.0, 0.0).T.astype(BF16)
    var_hot = jnp.where((sub < 12) & ((sub & 3) == var_row), 1.0, 0.0).T.astype(BF16)
    half = HEAD // 2
    step = iota((half, LANES), 0).astype(F32)
    angle = time_row.astype(F32) * jnp.exp(step * (-math.log(10000.0) / half))
    cosine, sine = jnp.cos(angle), jnp.sin(angle)
    cosine = jnp.concatenate([cosine] * 4, axis=0).T
    sine = jnp.concatenate([-sine, sine, -sine, sine], axis=0).T
    return time_hot, var_hot, cosine, sine


def own_tables(
    by_owner, heads, length, bias, time, var, cache_var, time_hot, var_hot, cosine, sine, mask, key_hot, shift
):
    first = first_chunk(by_owner)
    sub = iota((LANES, LANES), 0)
    cache_chunks = cache_var.shape[0]
    for chunk in range(cache_chunks):
        slot = sub + chunk * LANES
        mask[chunk] = jnp.where(slot >= length[0], MASKED, 0.0).astype(BF16)
        row = cache_var[chunk : chunk + 1, :]
        key_hot[chunk] = jnp.where((sub < 12) & ((sub & 3) == row), 1.0, 0.0).T.astype(BF16)
    for chunk in range(2):
        place = chunk if not by_owner else (first if chunk == 0 else 1 - first)
        time_row = time[pl.ds(place, 1), :]
        tables = row_tables(time_row, var[pl.ds(place, 1), :])
        time_hot[chunk], var_hot[chunk], cosine[chunk], sine[chunk] = tables
        key_hot[cache_chunks + chunk] = tables[1]
        later = jnp.where(time_row > (sub & (HEAD - 1)), MASKED, 0.0)
        mask[cache_chunks + chunk] = later.T.astype(BF16)
    lane = iota((1, LANES), 1)
    for head in range(heads):
        gain = jnp.full((1, LANES), (bias[0, head] - bias[1, head]) * LOG2E, F32)
        high, middle, low = (part.astype(F32) for part in three_parts(gain))
        row = jnp.where(lane < 4, high, jnp.where(lane < 8, middle, jnp.where(lane < 12, low, 0.0)))
        shift[head : head + 1, :] = row


def far_tables(by_owner, time, var, time_hot, var_hot, cosine, sine):
    first = first_chunk(by_owner)
    for chunk in range(2):
        place = chunk if not by_owner else (first if chunk == 0 else 1 - first)
        tables = row_tables(time[pl.ds(place, 1), :], var[pl.ds(place, 1), :])
        time_hot[chunk], var_hot[chunk], cosine[chunk], sine[chunk] = tables


def turned(values, cosine, sine):
    lane = iota(values.shape, 1)
    quarter = HEAD // 2
    other = jnp.where(
        (lane & (HEAD - 1)) < quarter,
        pltpu.roll(values, LANES - quarter, 1),
        pltpu.roll(values, quarter, 1),
    )
    return values * cosine + other * sine


def blocks(width):
    return [slice(start, start + LANES) for start in range(0, width, LANES)]


def project(first, second, weight, cosine, sine, queries, keys, values, rows):
    for chunk, block in enumerate((first, second)):
        rows[chunk * LANES : (chunk + 1) * LANES, :] = normed(block[...].astype(F32))
    for part, target in enumerate((queries, keys, values)):
        product = dot(rows[...], weight[part])
        for chunk in range(2):
            for cols in blocks(product.shape[1]):
                piece = product[chunk * LANES : (chunk + 1) * LANES, cols]
                if part < 2:
                    piece = turned(piece, cosine[chunk], sine[chunk])
                if part == 0:
                    piece = piece * (0.125 * LOG2E)
                target[chunk, :, cols] = piece.astype(BF16)


def attend_pair(pair, query, time_hot, var_hot, shift, keys, values, mask, key_hot):
    lane = iota((LANES, LANES), 1)
    key_lane = iota(keys.shape, 1)
    weighted, best = [], []
    for side in range(2):
        head = 2 * pair + side
        in_head = (lane < HEAD) if side == 0 else (lane >= HEAD)
        key_in_head = (key_lane < HEAD) if side == 0 else (key_lane >= HEAD)
        gain = shift[head : head + 1, :].astype(BF16)
        left = jnp.concatenate([jnp.where(in_head, query, time_hot), var_hot * gain], axis=1)
        right = jnp.concatenate([jnp.where(key_in_head, keys, mask), key_hot], axis=1)
        scores = dot(left, right, (1, 1))
        top = jnp.max(scores, axis=1, keepdims=True)
        weights = jnp.exp2(scores - top).astype(BF16)
        weighted.append(dot(weights, jnp.where(key_in_head, values, jnp.ones_like(values))))
        best.append(top)
    low = lane < HEAD
    total = pltpu.roll(jnp.where(low, weighted[1], weighted[0]), HEAD, 1)
    outputs = jnp.where(low, weighted[0], weighted[1]) / total
    return outputs, jnp.where(low, best[0], best[1]) + jnp.log2(total)


def key_block(index, cols, cache, fresh):
    return jnp.concatenate([cache[index, :, cols], fresh[0, :, cols], fresh[1, :, cols]], axis=0)


def attend_own(queries, time_hot, var_hot, shift, keys, values, cache, mask, key_hot, outputs, logs):
    all_mask = mask[...].reshape(-1, LANES)
    all_hot = key_hot[...].reshape(-1, LANES)
    for pair, cols in enumerate(blocks(queries.shape[2])):
        pair_keys = key_block(0, cols, cache, keys)
        pair_values = key_block(1, cols, cache, values)
        for chunk in range(2):
            out, log = attend_pair(
                pair, queries[chunk, :, cols], time_hot[chunk], var_hot[chunk], shift[...],
                pair_keys, pair_values, all_mask, all_hot,
            )
            outputs[chunk, :, cols] = out
            logs[chunk, :, cols] = log


def stat_place(part, width):
    count = width // LANES
    return part % count, (part // count) * (width // HEAD)


def attend_far(
    chunk, tokens, weight, cosine, sine, time_hot, var_hot, shift, keys, values, cache, mask, key_hot, message
):
    width = message.shape[1]
    product = dot(normed(tokens[...].astype(F32)), weight[0])
    all_mask = mask[...].reshape(-1, LANES)
    all_hot = key_hot[...].reshape(-1, LANES)
    stats = [jnp.zeros((STAT_ROWS, LANES), F32) for _ in blocks(width)]
    for pair, cols in enumerate(blocks(width)):
        query = turned(product[:, cols], cosine[chunk], sine[chunk]) * (0.125 * LOG2E)
        out, log = attend_pair(
            pair, query.astype(BF16), time_hot[chunk], var_hot[chunk], shift[...],
            key_block(0, cols, cache, keys), key_block(1, cols, cache, values), all_mask, all_hot,
        )
        message[:LANES, cols] = out.astype(BF16)
        row, lane = iota((STAT_ROWS, LANES), 0), iota((STAT_ROWS, LANES), 1)
        for part, piece in enumerate(three_parts(log)):
            block, offset = stat_place(part, width)
            pick = (row - offset - 2 * pair) * HEAD == lane
            stats[block] += dot(jnp.where(pick, 1.0, 0.0).astype(BF16), piece, (1, 1))
    for block, cols in zip(stats, blocks(width), strict=True):
        message[LANES:, cols] = block.astype(BF16)


def join(chunk, linked, own, own_log, message, weight, kept, sent):
    width = message.shape[1]
    pieces = []
    row = iota((STAT_ROWS, LANES), 0)
    lane = iota((STAT_ROWS, LANES), 1)
    for pair, cols in enumerate(blocks(width)):
        far_log = jnp.zeros((LANES, LANES), F32)
        for part in range(3):
            block, offset = stat_place(part, width)
            stat = message[LANES:, block * LANES : (block + 1) * LANES]
            pick = row - offset - 2 * pair == lane // HEAD
            far_log += dot(stat, jnp.where(pick, 1.0, 0.0).astype(BF16), (0, 0))
        far_log = jnp.where(linked[0] > 0, far_log, MASKED)
        share = 1.0 / (1.0 + jnp.exp2(far_log - own_log[chunk, :, cols]))
        far = message[:LANES, cols].astype(F32)
        pieces.append((far + (own[chunk, :, cols] - far) * share).astype(BF16))
    product = dot(jnp.concatenate(pieces, axis=1), weight[...])
    kept[...] = product
    sent[...] = product.astype(BF16)


def feed(final, tokens, kept, received, gate_up, down, out):
    stream = (tokens[...].astype(F32) + kept[...] + received[...].astype(F32)).astype(BF16)
    stream = stream.astype(F32)
    rows = normed(stream)
    gate = dot(rows, gate_up[0])
    hidden = (gate / (1.0 + jnp.exp(-gate)) * dot(rows, gate_up[1])).astype(BF16)
    product = dot(hidden, down[...])
    out[...] = stream + product if final else product.astype(BF16)


def shards(
    tokens,
    variate,
    time_ids,
    cache_var,
    cache_len,
    linked,
    cache_kv,
    var_bias,
    w_qkv,
    w_out,
    w_gate_up,
    w_down,
):
    heads = var_bias.shape[1]
    width = cache_kv.shape[2]
    model = tokens.shape[1]
    cache_rows = cache_kv.shape[1]
    ways = lax.axis_size("tp")
    partner = lax.axis_size("group") // 2
    paired = ways == 2
    chunk = (LANES, LANES)
    key_chunks = cache_rows // LANES + 2

    far_tokens = swap(tokens, "group", partner)
    time, var = time_ids.reshape(2, LANES), variate.reshape(2, LANES)
    far_time, far_var = (swap(ids, "group", partner) for ids in (time, var))
    if paired:
        own_rows = (tokens, swap(tokens, "tp", 1))
    else:
        gathered = lax.all_gather(tokens, "tp", axis=0, tiled=True)
        own_rows = (gathered[:LANES], gathered[LANES:])

    time_hot, var_hot, cosine, sine, mask, key_hot, shift = call(
        functools.partial(own_tables, paired, heads),
        [((2, *chunk), BF16), ((2, *chunk), BF16), ((2, *chunk), F32), ((2, *chunk), F32)]
        + [((key_chunks, *chunk), BF16), ((key_chunks, *chunk), BF16), ((heads, LANES), F32)],
        time, var, cache_var.reshape(-1, LANES), scalars=(cache_len, var_bias),
    )
    far_time_hot, far_var_hot, far_cosine, far_sine = call(
        functools.partial(far_tables, paired),
        [((2, *chunk), BF16), ((2, *chunk), BF16), ((2, *chunk), F32), ((2, *chunk), F32)],
        far_time, far_var,
    )
    queries, keys, values = call(
        project, [((2, LANES, width), BF16)] * 3,
        *own_rows, w_qkv, cosine, sine,
        flops=6 * 256 * model * width, scratch=[pltpu.VMEM((2 * LANES, model), BF16)],
    )
    if paired:
        far_rows = (far_tokens, swap(far_tokens, "tp", 1))
    else:
        gathered = lax.all_gather(far_tokens, "tp", axis=0, tiled=True)
        far_rows = (gathered[:LANES], gathered[LANES:])

    key_side = (shift, keys, values, cache_kv, mask, key_hot)
    own, own_log = call(
        attend_own, [((2, LANES, width), F32)] * 2,
        queries, time_hot, var_hot, *key_side, flops=4 * 256 * 768 * width * 4,
    )
    returned = []
    for index in range(2):
        (message,) = call(
            functools.partial(attend_far, index), [((LANES + STAT_ROWS, width), BF16)],
            far_rows[index], w_qkv, far_cosine, far_sine, far_time_hot, far_var_hot, *key_side,
            flops=4 * 128 * 768 * width * 4,
        )
        returned.append(swap(message, "group", partner))
    kept, sent = [], []
    for index in range(2):
        products = call(
            functools.partial(join, index), [((LANES, model), F32), ((LANES, model), BF16)],
            own, own_log, returned[index], w_out, scalars=(linked,), flops=2 * 128 * width * model,
        )
        kept.append(products[0])
        sent.append(products[1])

    def fed(index, final, part, received):
        (out,) = call(
            functools.partial(feed, final), [((LANES, model), F32 if final else BF16)],
            own_rows[index], part, received, w_gate_up, w_down,
            flops=6 * 128 * model * w_down.shape[0],
        )
        return out

    if paired:
        from_first = swap(sent[0], "tp", 1)
        from_second = swap(sent[1], "tp", 1)
        other = swap(fed(1, False, kept[1], from_first), "tp", 1)
        mine = fed(0, True, kept[0], from_second)
        return (mine + other.astype(F32)).astype(BF16)
    attended = [lax.psum(part, "tp") for part in sent]
    nothing = jnp.zeros((LANES, model), F32)
    parts = jnp.concatenate([fed(i, False, nothing, attended[i]) for i in range(2)])
    summed = lax.psum(parts, "tp")
    local = tokens.shape[0]
    start = lax.axis_index("tp") * local
    attended = lax.dynamic_slice_in_dim(jnp.concatenate(attended), start, local, 0)
    stream = (tokens.astype(F32) + attended.astype(F32)).astype(BF16).astype(F32)
    own_ffn = lax.dynamic_slice_in_dim(summed, start, local, 0).astype(F32)
    return (stream + own_ffn).astype(BF16)


def solution(mesh):
    return jax.shard_map(
        shards,
        mesh=mesh,
        in_specs=(
            P(("group", "tp"), None),
            P("group"),
            P("group"),
            P("group"),
            P("group"),
            P("group"),
            P(None, "group", "tp"),
            P(None, "tp"),
            P(None, None, "tp"),
            P("tp", None),
            P(None, None, "tp"),
            P("tp", None),
        ),
        out_specs=P(("group", "tp"), None),
        check_vma=False,
    )
```

```python
import functools
import math

import jax
import jax.numpy as jnp
from jax import lax
from jax.experimental import pallas as pl
from jax.experimental.pallas import tpu as pltpu
from jax.sharding import PartitionSpec as P

LANES = 128
HEAD = 64
HALF = HEAD // 2
LOG_ROWS = 8
STAT_ROWS = 32
LOG2E = math.log2(math.e)
MASKED = -1e30
F32 = jnp.float32
BF16 = jnp.bfloat16

IN_VMEM = pl.BlockSpec(memory_space=pltpu.VMEM)
IN_SMEM = pl.BlockSpec(memory_space=pltpu.SMEM)


def call(body, outs, *operands, scalars=(), flops=0, scratch=()):
    shapes = [jax.ShapeDtypeStruct(shape, dtype) for shape, dtype in outs]
    moved = sum(x.size * x.dtype.itemsize for x in operands)
    return pl.pallas_call(
        body,
        out_shape=shapes,
        in_specs=[IN_SMEM] * len(scalars) + [IN_VMEM] * len(operands),
        out_specs=[IN_VMEM] * len(shapes),
        scratch_shapes=list(scratch),
        cost_estimate=pl.CostEstimate(flops=flops, bytes_accessed=moved, transcendentals=0),
        compiler_params=pltpu.CompilerParams(vmem_limit_bytes=16 << 20),
    )(*scalars, *operands)


def swap(block, axis, distance):
    count = lax.axis_size(axis)
    return lax.ppermute(block, axis, [(i, i ^ distance) for i in range(count)])


def normed(values):
    return (values * lax.rsqrt(jnp.mean(values * values, axis=-1, keepdims=True) + 1e-05)).astype(
        BF16
    )


def iota(shape, dim):
    return lax.broadcasted_iota(jnp.int32, shape, dim)


def dot(a, b):
    return jnp.dot(a, b, preferred_element_type=F32)


def three_parts(value):
    high = value.astype(BF16).astype(F32)
    middle = (value - high).astype(BF16).astype(F32)
    low = (value - high - middle).astype(BF16).astype(F32)
    return high, middle, low


def blocks(width):
    return [slice(start, start + LANES) for start in range(0, width, LANES)]


def place_of(chunk, by_owner):
    if not by_owner:
        return chunk
    return lax.axis_index("tp") if chunk == 0 else 1 - lax.axis_index("tp")


def ids_of(small, chunk, by_owner):
    ids = small[pl.ds(place_of(chunk, by_owner), 1), :].astype(jnp.int32)
    return ids & (HEAD - 1), ids >> 6


def query_tables(time_row, var_row):
    time_hot = jnp.where(iota((HEAD, LANES), 0) == time_row, 1.0, 0.0).astype(BF16)
    sub = iota((16, LANES), 0)
    var_hot = jnp.where((sub < 12) & ((sub & 3) == var_row), 1.0, 0.0).astype(BF16)
    angle = time_row.astype(F32) * jnp.exp(
        iota((HALF, LANES), 0).astype(F32) * (-math.log(10000.0) / HALF)
    )
    return time_hot, var_hot, jnp.cos(angle), jnp.sin(angle)


def key_table(hidden, var_row):
    sub = iota((LANES - HEAD, LANES), 0)
    same = jnp.where((sub < 12) & ((sub & 3) == var_row), 1.0, 0.0)
    return jnp.concatenate([jnp.where(hidden, MASKED, 0.0), same], axis=0).T.astype(BF16)


def tables(
    by_owner, heads, length, small, time_hot, var_hot, cosine, sine, key_cosine, key_sine, key_hot, gains
):
    cache_chunks = key_hot.shape[0] - 2
    for chunk in range(cache_chunks):
        slot = iota((HEAD, LANES), 1) + chunk * LANES
        cache_var = small[chunk + 2 : chunk + 3, :].astype(jnp.int32)
        key_hot[chunk] = key_table(slot >= length[0], cache_var)
    for chunk in range(2):
        time_row, var_row = ids_of(small, chunk, by_owner)
        time_hot[chunk], var_hot[chunk], cos, sin = query_tables(time_row, var_row)
        cosine[chunk], sine[chunk] = cos, sin
        key_cosine[chunk] = jnp.concatenate([cos] * 4, axis=0).T
        key_sine[chunk] = jnp.concatenate([-sin, sin, -sin, sin], axis=0).T
        key_hot[cache_chunks + chunk] = key_table(time_row > iota((HEAD, LANES), 0), var_row)
    sub = iota((16, LANES), 0)
    bias = small[cache_chunks + 2 : cache_chunks + 3, :] * LOG2E
    for head in range(heads):
        gain = bias[:, head : head + 1] - bias[:, heads + head : heads + head + 1]
        high, middle, low = three_parts(jnp.broadcast_to(gain, (16, LANES)))
        gains[head] = jnp.where(sub < 4, high, jnp.where(sub < 8, middle, low)).astype(BF16)


def arrange(cache, cache_values):
    for rows in blocks(cache.shape[1]):
        for cols in blocks(cache.shape[2]):
            cache_values[cols, rows] = cache[1, rows, cols].T


def turn_queries(piece, cosine, sine):
    turned = []
    for start in range(0, LANES, HEAD):
        x, y = piece[start : start + HALF, :], piece[start + HALF : start + HEAD, :]
        turned += [x * cosine - y * sine, y * cosine + x * sine]
    return (jnp.concatenate(turned, axis=0) * (0.125 * LOG2E)).astype(BF16)


def turn_keys(piece, cosine, sine):
    first = (iota(piece.shape, 1) & (HEAD - 1)) < HALF
    other = jnp.where(first, pltpu.roll(piece, LANES - HALF, 1), pltpu.roll(piece, HALF, 1))
    return (piece * cosine + other * sine).astype(BF16)


def project(
    first, second, weight, cosine, sine, key_cosine, key_sine, queries, keys, values, rows
):
    for chunk, block in enumerate((first, second)):
        rows[chunk * LANES : (chunk + 1) * LANES, :] = normed(block[...].astype(F32))
    for part in (1, 0, 2):
        product = dot(rows[...], weight[part])
        for chunk in range(2):
            for cols in blocks(product.shape[1]):
                piece = product[chunk * LANES : (chunk + 1) * LANES, cols]
                if part == 0:
                    queries[chunk, cols, :] = turn_queries(piece.T, cosine[chunk], sine[chunk])
                elif part == 1:
                    keys[chunk, :, cols] = turn_keys(piece, key_cosine[chunk], key_sine[chunk])
                else:
                    values[chunk, cols, :] = piece.T.astype(BF16)


def attend(queries, time_hot, var_hot, gains, keys, values, cache, cache_values, key_hot, emit):
    hot = key_hot[...].reshape(-1, LANES)
    ones = jnp.ones((16, hot.shape[0]), BF16)
    blank = jnp.zeros((HEAD, LANES), BF16)
    rest = jnp.zeros((LANES - HEAD - 16, LANES), BF16)
    chunks, width = len(queries), cache_values.shape[0]
    units = [(pair, chunk) for pair in range(width // LANES) for chunk in range(chunks)]
    left, right = [], []
    for cols in blocks(width):
        block = [cache[0, :, cols], keys[0, :, cols], keys[1, :, cols]]
        left.append(jnp.concatenate([jnp.concatenate(block, axis=0), hot], axis=1))
        block = [cache_values[cols, :], values[0, cols, :], values[1, cols, :]]
        right.append(jnp.concatenate([jnp.concatenate(block, axis=1), ones], axis=0))

    def features(pair, chunk):
        sides = []
        for side in range(2):
            head = 2 * pair + side
            query = queries[chunk][head * HEAD : (head + 1) * HEAD, :]
            both = [query, blank] if side == 0 else [blank, query]
            sides.append(
                jnp.concatenate(
                    both + [time_hot[chunk], var_hot[chunk] * gains[head], rest], axis=0
                )
            )
        return jnp.concatenate(sides, axis=1)

    scores, weights = {}, {}
    for step in range(len(units) + 2):
        if step < len(units):
            pair, chunk = units[step]
            scores[step] = dot(left[pair], features(pair, chunk))
        if 0 <= step - 1 < len(units):
            score = scores.pop(step - 1)
            top = jnp.max(score, axis=0, keepdims=True)
            weights[step - 1] = jnp.exp2(score - top).astype(BF16), top
        if 0 <= step - 2 < len(units):
            pair, chunk = units[step - 2]
            weight, top = weights.pop(step - 2)
            product = dot(right[pair], weight)
            for side in range(2):
                head, lanes = 2 * pair + side, slice(side * LANES, (side + 1) * LANES)
                total = product[LANES : LANES + 1, lanes]
                out = product[side * HEAD : (side + 1) * HEAD, lanes] * (1.0 / total)
                emit(chunk, head, out, top[:, lanes] + jnp.log2(total))


def attend_own(
    queries, time_hot, var_hot, gains, keys, values, cache, cache_values, key_hot, outputs, logs
):
    def emit(chunk, head, out, log):
        outputs[chunk, head * HEAD : (head + 1) * HEAD, :] = out
        logs[chunk, head : head + 1, :] = log

    rows = [queries.at[chunk] for chunk in range(2)]
    attend(
        rows, time_hot, var_hot, gains, keys, values, cache, cache_values, key_hot, emit
    )


def attend_far(
    chunk, by_owner, small, tokens, weight, gains, keys, values, cache, cache_values, key_hot, message, queries, logs
):
    width = cache_values.shape[0]
    time_hot, var_hot, cosine, sine = query_tables(*ids_of(small, chunk, by_owner))
    product = dot(normed(tokens[...].astype(F32)), weight[0])
    for cols in blocks(width):
        queries[cols, :] = turn_queries(product[:, cols].T, cosine, sine)
    logs[...] = jnp.zeros_like(logs)

    def emit(_, head, out, log):
        message[head * HEAD : (head + 1) * HEAD, :] = out.astype(BF16)
        logs[head : head + 1, :] = log

    attend(
        [queries], [time_hot], [var_hot], gains, keys, values, cache, cache_values, key_hot, emit
    )
    parts = list(three_parts(logs[...])) + [jnp.zeros((LOG_ROWS, LANES), F32)]
    message[width:, :] = jnp.concatenate(parts, axis=0).astype(BF16)


def join(chunk, linked, own, own_log, message, weight, kept, sent):
    width = weight.shape[0]
    stats = message[width:, :].astype(F32)
    far_log = stats[:8, :] + stats[8:16, :] + stats[16:24, :]
    far_log = jnp.where(linked[0] > 0, far_log, MASKED)
    share = 1.0 / (1.0 + jnp.exp2(far_log - own_log[chunk]))
    pieces = []
    for cols in blocks(width):
        joined = []
        for start in range(cols.start, cols.stop, HEAD):
            rows, head = slice(start, start + HEAD), start // HEAD
            far = message[rows, :].astype(F32)
            joined.append(far + (own[chunk, rows, :] - far) * share[head : head + 1, :])
        pieces.append(jnp.concatenate(joined, axis=0).T.astype(BF16))
    product = dot(jnp.concatenate(pieces, axis=1), weight[...])
    kept[...] = product
    sent[...] = product.astype(BF16)


def feed(final, tokens, kept, received, gate_up, down, out):
    stream = (tokens[...].astype(F32) + kept[...] + received[...].astype(F32)).astype(BF16)
    stream = stream.astype(F32)
    rows = normed(stream)
    gate = dot(rows, gate_up[0])
    hidden = (gate / (1.0 + jnp.exp(-gate)) * dot(rows, gate_up[1])).astype(BF16)
    product = dot(hidden, down[...])
    out[...] = stream + product if final else product.astype(BF16)


def shards(
    tokens,
    variate,
    time_ids,
    cache_var,
    cache_len,
    linked,
    cache_kv,
    var_bias,
    w_qkv,
    w_out,
    w_gate_up,
    w_down,
):
    heads = var_bias.shape[1]
    width = cache_kv.shape[2]
    model = tokens.shape[1]
    cache_rows = cache_kv.shape[1]
    ways = lax.axis_size("tp")
    partner = lax.axis_size("group") // 2
    paired = ways == 2
    key_chunks = cache_rows // LANES + 2

    far_tokens = swap(tokens, "group", partner)
    ids, held = lax.optimization_barrier(((time_ids + HEAD * variate).astype(F32), tokens))
    if paired:
        other_tokens = swap(held, "tp", 1)
    small = jnp.concatenate(
        [
            ids,
            cache_var.astype(F32),
            jnp.pad(var_bias.reshape(-1), (0, LANES - 2 * heads)),
        ]
    ).reshape(-1, LANES)
    far_small = swap(small, "group", partner)
    time_hot, var_hot, cosine, sine, key_cosine, key_sine, key_hot, gains = call(
        functools.partial(tables, paired, heads),
        [((2, HEAD, LANES), BF16), ((2, 16, LANES), BF16), ((2, HALF, LANES), F32), ((2, HALF, LANES), F32)]
        + [((2, LANES, LANES), F32)] * 2
        + [((key_chunks, LANES, LANES), BF16), ((heads, 16, LANES), BF16)],
        small, scalars=(cache_len,), flops=6_000_000_000,
    )
    (cache_values,) = call(arrange, [((width, cache_rows), BF16)], cache_kv)

    def all_rows(mine, other):
        if paired:
            return mine, other
        gathered = lax.all_gather(mine, "tp", axis=0, tiled=True)
        return gathered[:LANES], gathered[LANES:]

    own_rows = all_rows(tokens, other_tokens if paired else None)
    queries, keys, values = call(
        project,
        [((2, width, LANES), BF16), ((2, LANES, width), BF16), ((2, width, LANES), BF16)],
        *own_rows, w_qkv, cosine, sine, key_cosine, key_sine,
        flops=6 * 256 * model * width, scratch=[pltpu.VMEM((2 * LANES, model), BF16)],
    )
    key_side = (gains, keys, values, cache_kv, cache_values, key_hot)
    own, own_log = call(
        attend_own, [((2, width, LANES), F32), ((2, LOG_ROWS, LANES), F32)],
        queries, time_hot, var_hot, *key_side, flops=8 * 256 * 768 * width,
    )
    far_tokens, far_small, own = lax.optimization_barrier((far_tokens, far_small, own))
    far_rows = all_rows(far_tokens, swap(far_tokens, "tp", 1) if paired else None)
    messages = []
    for index in range(2):
        (message,) = call(
            functools.partial(attend_far, index, paired), [((width + STAT_ROWS, LANES), BF16)],
            far_small, far_rows[index], w_qkv, *key_side, flops=8 * 128 * 768 * width,
            scratch=[pltpu.VMEM((width, LANES), BF16), pltpu.VMEM((LOG_ROWS, LANES), F32)],
        )
        messages.append(message)
    returned = [swap(message, "group", partner) for message in messages]
    returned[0], _ = lax.optimization_barrier((returned[0], messages[1]))
    kept, sent = [], []
    for index in range(2):
        products = call(
            functools.partial(join, index), [((LANES, model), F32), ((LANES, model), BF16)],
            own, own_log, returned[index], w_out, scalars=(linked,), flops=2 * 128 * width * model,
        )
        kept.append(products[0])
        sent.append(products[1])

    def fed(index, final, part, received):
        (out,) = call(
            functools.partial(feed, final), [((LANES, model), F32 if final else BF16)],
            own_rows[index], part, received, w_gate_up, w_down,
            flops=6 * 128 * model * w_down.shape[0],
        )
        return out

    if paired:
        from_first = swap(sent[0], "tp", 1)
        from_second = swap(sent[1], "tp", 1)
        other = swap(fed(1, False, kept[1], from_first), "tp", 1)
        mine = fed(0, True, kept[0], from_second)
        return (mine + other.astype(F32)).astype(BF16)
    attended = [lax.psum(part, "tp") for part in sent]
    nothing = jnp.zeros((LANES, model), F32)
    parts = jnp.concatenate([fed(i, False, nothing, attended[i]) for i in range(2)])
    summed = lax.psum(parts, "tp")
    local = tokens.shape[0]
    start = lax.axis_index("tp") * local
    attended = lax.dynamic_slice_in_dim(jnp.concatenate(attended), start, local, 0)
    stream = (tokens.astype(F32) + attended.astype(F32)).astype(BF16).astype(F32)
    own_ffn = lax.dynamic_slice_in_dim(summed, start, local, 0).astype(F32)
    return (stream + own_ffn).astype(BF16)


def solution(mesh):
    return jax.shard_map(
        shards,
        mesh=mesh,
        in_specs=(
            P(("group", "tp"), None),
            P("group"),
            P("group"),
            P("group"),
            P("group"),
            P("group"),
            P(None, "group", "tp"),
            P(None, "tp"),
            P(None, None, "tp"),
            P("tp", None),
            P(None, None, "tp"),
            P("tp", None),
        ),
        out_specs=P(("group", "tp"), None),
        check_vma=False,
    )
```

```python
import functools
import math

import jax
import jax.numpy as jnp
from jax import lax
from jax.experimental import pallas as pl
from jax.experimental.pallas import tpu as pltpu
from jax.sharding import PartitionSpec as P

LANES = 128
HEAD = 64
HALF = HEAD // 2
LOG_ROWS = 8
STAT_ROWS = 32
LOG2E = math.log2(math.e)
MASKED = -1e30
F32 = jnp.float32
BF16 = jnp.bfloat16

IN_VMEM = pl.BlockSpec(memory_space=pltpu.VMEM)
IN_SMEM = pl.BlockSpec(memory_space=pltpu.SMEM)


def call(body, outs, *operands, scalars=(), flops=0, scratch=()):
    shapes = [jax.ShapeDtypeStruct(shape, dtype) for shape, dtype in outs]
    moved = sum(x.size * x.dtype.itemsize for x in operands)
    return pl.pallas_call(
        body,
        out_shape=shapes,
        in_specs=[IN_SMEM] * len(scalars) + [IN_VMEM] * len(operands),
        out_specs=[IN_VMEM] * len(shapes),
        scratch_shapes=list(scratch),
        cost_estimate=pl.CostEstimate(flops=flops, bytes_accessed=moved, transcendentals=0),
        compiler_params=pltpu.CompilerParams(vmem_limit_bytes=16 << 20),
    )(*scalars, *operands)


def swap(block, axis, distance):
    count = lax.axis_size(axis)
    return lax.ppermute(block, axis, [(i, i ^ distance) for i in range(count)])


def normed(values):
    return (values * lax.rsqrt(jnp.mean(values * values, axis=-1, keepdims=True) + 1e-05)).astype(
        BF16
    )


def iota(shape, dim):
    return lax.broadcasted_iota(jnp.int32, shape, dim)


def dot(a, b):
    return jnp.dot(a, b, preferred_element_type=F32)


def three_parts(value):
    high = value.astype(BF16).astype(F32)
    middle = (value - high).astype(BF16).astype(F32)
    low = (value - high - middle).astype(BF16).astype(F32)
    return high, middle, low


def blocks(width):
    return [slice(start, start + LANES) for start in range(0, width, LANES)]


def place_of(chunk, by_owner):
    if not by_owner:
        return chunk
    return lax.axis_index("tp") if chunk == 0 else 1 - lax.axis_index("tp")


def ids_of(small, chunk, by_owner):
    ids = small[pl.ds(place_of(chunk, by_owner), 1), :].astype(jnp.int32)
    return ids & (HEAD - 1), ids >> 6


def query_tables(time_row, var_row):
    time_hot = jnp.where(iota((HEAD, LANES), 0) == time_row, 1.0, 0.0).astype(BF16)
    sub = iota((16, LANES), 0)
    var_hot = jnp.where((sub < 12) & ((sub & 3) == var_row), 1.0, 0.0).astype(BF16)
    angle = time_row.astype(F32) * jnp.exp(
        iota((HALF, LANES), 0).astype(F32) * (-math.log(10000.0) / HALF)
    )
    return time_hot, var_hot, jnp.cos(angle), jnp.sin(angle)


def key_table(hidden, var_row):
    sub = iota((LANES - HEAD, LANES), 0)
    same = jnp.where((sub < 12) & ((sub & 3) == var_row), 1.0, 0.0)
    return jnp.concatenate([jnp.where(hidden, MASKED, 0.0), same], axis=0).T.astype(BF16)


def tables(
    by_owner, heads, length, small, time_hot, var_hot, cosine, sine, key_cosine, key_sine, key_hot, gains
):
    cache_chunks = key_hot.shape[0] - 2
    for chunk in range(cache_chunks):
        slot = iota((HEAD, LANES), 1) + chunk * LANES
        cache_var = small[chunk + 2 : chunk + 3, :].astype(jnp.int32)
        key_hot[chunk] = key_table(slot >= length[0], cache_var)
    for chunk in range(2):
        time_row, var_row = ids_of(small, chunk, by_owner)
        time_hot[chunk], var_hot[chunk], cos, sin = query_tables(time_row, var_row)
        cosine[chunk], sine[chunk] = cos, sin
        key_cosine[chunk] = jnp.concatenate([cos] * 4, axis=0).T
        key_sine[chunk] = jnp.concatenate([-sin, sin, -sin, sin], axis=0).T
        key_hot[cache_chunks + chunk] = key_table(time_row > iota((HEAD, LANES), 0), var_row)
    sub = iota((16, LANES), 0)
    bias = small[cache_chunks + 2 : cache_chunks + 3, :] * LOG2E
    for head in range(heads):
        gain = bias[:, head : head + 1] - bias[:, heads + head : heads + head + 1]
        high, middle, low = three_parts(jnp.broadcast_to(gain, (16, LANES)))
        gains[head] = jnp.where(sub < 4, high, jnp.where(sub < 8, middle, low)).astype(BF16)


def arrange(cache, cache_values):
    for rows in blocks(cache.shape[1]):
        for cols in blocks(cache.shape[2]):
            cache_values[cols, rows] = cache[1, rows, cols].T


def turn_queries(piece, cosine, sine):
    turned = []
    for start in range(0, LANES, HEAD):
        x, y = piece[start : start + HALF, :], piece[start + HALF : start + HEAD, :]
        turned += [x * cosine - y * sine, y * cosine + x * sine]
    return (jnp.concatenate(turned, axis=0) * (0.125 * LOG2E)).astype(BF16)


def turn_keys(piece, cosine, sine):
    first = (iota(piece.shape, 1) & (HEAD - 1)) < HALF
    other = jnp.where(first, pltpu.roll(piece, LANES - HALF, 1), pltpu.roll(piece, HALF, 1))
    return (piece * cosine + other * sine).astype(BF16)


def project(
    first, second, weight, cosine, sine, key_cosine, key_sine, queries, keys, values, rows
):
    for chunk, block in enumerate((first, second)):
        rows[chunk * LANES : (chunk + 1) * LANES, :] = normed(block[...].astype(F32))
    for part in (1, 0, 2):
        product = dot(rows[...], weight[part])
        for chunk in range(2):
            for cols in blocks(product.shape[1]):
                piece = product[chunk * LANES : (chunk + 1) * LANES, cols]
                if part == 0:
                    queries[chunk, cols, :] = turn_queries(piece.T, cosine[chunk], sine[chunk])
                elif part == 1:
                    keys[chunk, :, cols] = turn_keys(piece, key_cosine[chunk], key_sine[chunk])
                else:
                    values[chunk, cols, :] = piece.T.astype(BF16)


def attend(queries, time_hot, var_hot, gains, keys, values, cache, cache_values, key_hot, emit):
    hot = key_hot[...].reshape(-1, LANES)
    ones = jnp.ones((16, hot.shape[0]), BF16)
    blank = jnp.zeros((HEAD, LANES), BF16)
    rest = jnp.zeros((LANES - HEAD - 16, LANES), BF16)
    chunks, width = len(queries), cache_values.shape[0]
    units = [(pair, chunk) for pair in range(width // LANES) for chunk in range(chunks)]
    left, right = [], []
    for cols in blocks(width):
        block = [cache[0, :, cols], keys[0, :, cols], keys[1, :, cols]]
        left.append(jnp.concatenate([jnp.concatenate(block, axis=0), hot], axis=1))
        block = [cache_values[cols, :], values[0, cols, :], values[1, cols, :]]
        right.append(jnp.concatenate([jnp.concatenate(block, axis=1), ones], axis=0))

    def features(pair, chunk):
        sides = []
        for side in range(2):
            head = 2 * pair + side
            query = queries[chunk][head * HEAD : (head + 1) * HEAD, :]
            both = [query, blank] if side == 0 else [blank, query]
            sides.append(
                jnp.concatenate(
                    both + [time_hot[chunk], var_hot[chunk] * gains[head], rest], axis=0
                )
            )
        return jnp.concatenate(sides, axis=1)

    scores, weights = {}, {}
    for step in range(len(units) + 2):
        if step < len(units):
            pair, chunk = units[step]
            scores[step] = dot(left[pair], features(pair, chunk))
        if 0 <= step - 1 < len(units):
            score = scores.pop(step - 1)
            top = jnp.max(score, axis=0, keepdims=True)
            weights[step - 1] = jnp.exp2(score - top).astype(BF16), top
        if 0 <= step - 2 < len(units):
            pair, chunk = units[step - 2]
            weight, top = weights.pop(step - 2)
            product = dot(right[pair], weight)
            for side in range(2):
                head, lanes = 2 * pair + side, slice(side * LANES, (side + 1) * LANES)
                total = product[LANES : LANES + 1, lanes]
                out = product[side * HEAD : (side + 1) * HEAD, lanes] * (1.0 / total)
                emit(chunk, head, out, top[:, lanes] + jnp.log2(total))


def attend_own(
    queries, time_hot, var_hot, gains, keys, values, cache, cache_values, key_hot, outputs, logs
):
    def emit(chunk, head, out, log):
        outputs[chunk, head * HEAD : (head + 1) * HEAD, :] = out
        logs[chunk, head : head + 1, :] = log

    rows = [queries.at[chunk] for chunk in range(2)]
    attend(
        rows, time_hot, var_hot, gains, keys, values, cache, cache_values, key_hot, emit
    )


def attend_far(
    chunk, by_owner, small, tokens, weight, gains, keys, values, cache, cache_values, key_hot, message, queries, logs
):
    width = cache_values.shape[0]
    time_hot, var_hot, cosine, sine = query_tables(*ids_of(small, chunk, by_owner))
    product = dot(normed(tokens[...].astype(F32)), weight[0])
    for cols in blocks(width):
        queries[cols, :] = turn_queries(product[:, cols].T, cosine, sine)
    logs[...] = jnp.zeros_like(logs)

    def emit(_, head, out, log):
        message[head * HEAD : (head + 1) * HEAD, :] = out.astype(BF16)
        logs[head : head + 1, :] = log

    attend(
        [queries], [time_hot], [var_hot], gains, keys, values, cache, cache_values, key_hot, emit
    )
    parts = list(three_parts(logs[...])) + [jnp.zeros((LOG_ROWS, LANES), F32)]
    message[width:, :] = jnp.concatenate(parts, axis=0).astype(BF16)


def join(chunk, own, own_log, *refs):
    *linked, weight, kept, sent = refs
    width = weight.shape[0]
    if linked:
        (message,) = linked
        stats = message[width:, :].astype(F32)
        far_log = stats[:8, :] + stats[8:16, :] + stats[16:24, :]
        share = 1.0 / (1.0 + jnp.exp2(far_log - own_log[chunk]))
    pieces = []
    for cols in blocks(width):
        joined = []
        for start in range(cols.start, cols.stop, HEAD):
            rows, head = slice(start, start + HEAD), start // HEAD
            part = own[chunk, rows, :]
            if linked:
                far = message[rows, :].astype(F32)
                part = far + (part - far) * share[head : head + 1, :]
            joined.append(part)
        pieces.append(jnp.concatenate(joined, axis=0).T.astype(BF16))
    product = dot(jnp.concatenate(pieces, axis=1), weight[...])
    kept[...] = product
    sent[...] = product.astype(BF16)


def feed(final, tokens, kept, received, gate_up, down, out):
    stream = (tokens[...].astype(F32) + kept[...] + received[...].astype(F32)).astype(BF16)
    stream = stream.astype(F32)
    rows = normed(stream)
    gate = dot(rows, gate_up[0])
    hidden = (gate / (1.0 + jnp.exp(-gate)) * dot(rows, gate_up[1])).astype(BF16)
    product = dot(hidden, down[...])
    out[...] = stream + product if final else product.astype(BF16)


def layer(
    with_partner,
    tokens,
    variate,
    time_ids,
    cache_var,
    cache_len,
    cache_kv,
    var_bias,
    w_qkv,
    w_out,
    w_gate_up,
    w_down,
):
    heads = var_bias.shape[1]
    width = cache_kv.shape[2]
    model = tokens.shape[1]
    cache_rows = cache_kv.shape[1]
    ways = lax.axis_size("tp")
    partner = lax.axis_size("group") // 2
    paired = ways == 2
    key_chunks = cache_rows // LANES + 2

    if with_partner:
        far_tokens = swap(tokens, "group", partner)
    if paired:
        other_tokens = swap(tokens, "tp", 1)
    small = jnp.concatenate(
        [
            (time_ids + HEAD * variate).astype(F32),
            cache_var.astype(F32),
            jnp.pad(var_bias.reshape(-1), (0, LANES - 2 * heads)),
        ]
    ).reshape(-1, LANES)
    if with_partner:
        far_small = swap(small, "group", partner)
    time_hot, var_hot, cosine, sine, key_cosine, key_sine, key_hot, gains = call(
        functools.partial(tables, paired, heads),
        [((2, HEAD, LANES), BF16), ((2, 16, LANES), BF16), ((2, HALF, LANES), F32), ((2, HALF, LANES), F32)]
        + [((2, LANES, LANES), F32)] * 2
        + [((key_chunks, LANES, LANES), BF16), ((heads, 16, LANES), BF16)],
        small, scalars=(cache_len,), flops=6_000_000_000,
    )
    (cache_values,) = call(arrange, [((width, cache_rows), BF16)], cache_kv)

    def all_rows(mine, other):
        if paired:
            return mine, other
        gathered = lax.all_gather(mine, "tp", axis=0, tiled=True)
        return gathered[:LANES], gathered[LANES:]

    own_rows = all_rows(tokens, other_tokens if paired else None)
    queries, keys, values = call(
        project,
        [((2, width, LANES), BF16), ((2, LANES, width), BF16), ((2, width, LANES), BF16)],
        *own_rows, w_qkv, cosine, sine, key_cosine, key_sine,
        flops=6 * 256 * model * width, scratch=[pltpu.VMEM((2 * LANES, model), BF16)],
    )
    key_side = (gains, keys, values, cache_kv, cache_values, key_hot)
    messages = []
    if with_partner:
        far_tokens, far_small, _ = lax.optimization_barrier((far_tokens, far_small, queries))
        far_rows = all_rows(far_tokens, swap(far_tokens, "tp", 1) if paired else None)

        def attended_for(index):
            (message,) = call(
                functools.partial(attend_far, index, paired), [((width + STAT_ROWS, LANES), BF16)],
                far_small, far_rows[index], w_qkv, *key_side, flops=8 * 128 * 768 * width,
                scratch=[pltpu.VMEM((width, LANES), BF16), pltpu.VMEM((LOG_ROWS, LANES), F32)],
            )
            return message

        messages.append(attended_for(0))
        queries, _ = lax.optimization_barrier((queries, messages[0]))
    own, own_log = call(
        attend_own, [((2, width, LANES), F32), ((2, LOG_ROWS, LANES), F32)],
        queries, time_hot, var_hot, *key_side, flops=8 * 256 * 768 * width,
    )
    if with_partner:
        far_small, _ = lax.optimization_barrier((far_small, own_log))
        messages.append(attended_for(1))
        returned = [swap(message, "group", partner) for message in messages]
        returned[0], _ = lax.optimization_barrier((returned[0], messages[1]))
    kept, sent = [], []
    for index in range(2):
        extra = [returned[index]] if with_partner else []
        products = call(
            functools.partial(join, index), [((LANES, model), F32), ((LANES, model), BF16)],
            own, own_log, *extra, w_out, flops=8_000_000_000,
        )
        kept.append(products[0])
        sent.append(products[1])

    def fed(index, final, part, received):
        (out,) = call(
            functools.partial(feed, final), [((LANES, model), F32 if final else BF16)],
            own_rows[index], part, received, w_gate_up, w_down,
            flops=6 * 128 * model * w_down.shape[0],
        )
        return out

    if paired:
        from_first = swap(sent[0], "tp", 1)
        from_second = swap(sent[1], "tp", 1)
        other = swap(fed(1, False, kept[1], from_first), "tp", 1)
        mine = fed(0, True, kept[0], from_second)
        return (mine + other.astype(F32)).astype(BF16)
    attended = [lax.psum(part, "tp") for part in sent]
    nothing = jnp.zeros((LANES, model), F32)
    parts = jnp.concatenate([fed(i, False, nothing, attended[i]) for i in range(2)])
    summed = lax.psum(parts, "tp")
    local = tokens.shape[0]
    start = lax.axis_index("tp") * local
    attended = lax.dynamic_slice_in_dim(jnp.concatenate(attended), start, local, 0)
    stream = (tokens.astype(F32) + attended.astype(F32)).astype(BF16).astype(F32)
    own_ffn = lax.dynamic_slice_in_dim(summed, start, local, 0).astype(F32)
    return (stream + own_ffn).astype(BF16)


def shards(tokens, variate, time_ids, cache_var, cache_len, linked, *rest):
    return lax.cond(
        linked[0] > 0,
        functools.partial(layer, True),
        functools.partial(layer, False),
        tokens, variate, time_ids, cache_var, cache_len, *rest,
    )


def solution(mesh):
    return jax.shard_map(
        shards,
        mesh=mesh,
        in_specs=(
            P(("group", "tp"), None),
            P("group"),
            P("group"),
            P("group"),
            P("group"),
            P("group"),
            P(None, "group", "tp"),
            P(None, "tp"),
            P(None, None, "tp"),
            P("tp", None),
            P(None, None, "tp"),
            P("tp", None),
        ),
        out_specs=P(("group", "tp"), None),
        check_vma=False,
    )
```

```python
import functools
import math

import jax
import jax.numpy as jnp
from jax import lax
from jax.experimental import pallas as pl
from jax.experimental.pallas import tpu as pltpu
from jax.sharding import PartitionSpec as P

LANES = 128
HEAD = 64
HALF = HEAD // 2
LOG_ROWS = 8
STAT_ROWS = 32
LOG2E = math.log2(math.e)
MASKED = -1e30
F32 = jnp.float32
BF16 = jnp.bfloat16

IN_VMEM = pl.BlockSpec(memory_space=pltpu.VMEM)
IN_SMEM = pl.BlockSpec(memory_space=pltpu.SMEM)


def call(body, outs, *operands, scalars=(), early=(), flops=0, scratch=()):
    if early:
        taken = len(scalars) + len(operands)
        inner = body

        def body(*refs):
            inner(*refs[:taken], *refs[taken + len(early) :])

        operands = (*operands, *early)
    shapes = [jax.ShapeDtypeStruct(shape, dtype) for shape, dtype in outs]
    moved = sum(x.size * x.dtype.itemsize for x in operands)
    return pl.pallas_call(
        body,
        out_shape=shapes,
        in_specs=[IN_SMEM] * len(scalars) + [IN_VMEM] * len(operands),
        out_specs=[IN_VMEM] * len(shapes),
        scratch_shapes=list(scratch),
        cost_estimate=pl.CostEstimate(flops=flops, bytes_accessed=moved, transcendentals=0),
        compiler_params=pltpu.CompilerParams(vmem_limit_bytes=16 << 20),
    )(*scalars, *operands)


def swap(block, axis, distance):
    count = lax.axis_size(axis)
    return lax.ppermute(block, axis, [(i, i ^ distance) for i in range(count)])


def normed(values):
    return (values * lax.rsqrt(jnp.mean(values * values, axis=-1, keepdims=True) + 1e-05)).astype(
        BF16
    )


def iota(shape, dim):
    return lax.broadcasted_iota(jnp.int32, shape, dim)


def dot(a, b):
    return jnp.dot(a, b, preferred_element_type=F32)


def three_parts(value):
    high = value.astype(BF16).astype(F32)
    middle = (value - high).astype(BF16).astype(F32)
    low = (value - high - middle).astype(BF16).astype(F32)
    return high, middle, low


def blocks(width):
    return [slice(start, start + LANES) for start in range(0, width, LANES)]


def place_of(chunk, by_owner):
    if not by_owner:
        return chunk
    return lax.axis_index("tp") if chunk == 0 else 1 - lax.axis_index("tp")


def ids_of(small, chunk, by_owner):
    ids = small[pl.ds(place_of(chunk, by_owner), 1), :].astype(jnp.int32)
    return ids & (HEAD - 1), ids >> 6


def query_tables(time_row, var_row):
    time_hot = jnp.where(iota((HEAD, LANES), 0) == time_row, 1.0, 0.0).astype(BF16)
    sub = iota((16, LANES), 0)
    var_hot = jnp.where((sub < 12) & ((sub & 3) == var_row), 1.0, 0.0).astype(BF16)
    angle = time_row.astype(F32) * jnp.exp(
        iota((HALF, LANES), 0).astype(F32) * (-math.log(10000.0) / HALF)
    )
    return time_hot, var_hot, jnp.cos(angle), jnp.sin(angle)


def key_table(hidden, var_row):
    sub = iota((LANES - HEAD, LANES), 0)
    same = jnp.where((sub < 12) & ((sub & 3) == var_row), 1.0, 0.0)
    return jnp.concatenate([jnp.where(hidden, MASKED, 0.0), same], axis=0).T.astype(BF16)


def tables(
    by_owner, heads, length, small, time_hot, var_hot, cosine, sine, key_cosine, key_sine, key_hot, gains
):
    cache_chunks = key_hot.shape[0] - 2
    for chunk in range(cache_chunks):
        slot = iota((HEAD, LANES), 1) + chunk * LANES
        cache_var = small[chunk + 2 : chunk + 3, :].astype(jnp.int32)
        key_hot[chunk] = key_table(slot >= length[0], cache_var)
    for chunk in range(2):
        time_row, var_row = ids_of(small, chunk, by_owner)
        time_hot[chunk], var_hot[chunk], cos, sin = query_tables(time_row, var_row)
        cosine[chunk], sine[chunk] = cos, sin
        key_cosine[chunk] = jnp.concatenate([cos] * 4, axis=0).T
        key_sine[chunk] = jnp.concatenate([-sin, sin, -sin, sin], axis=0).T
        key_hot[cache_chunks + chunk] = key_table(time_row > iota((HEAD, LANES), 0), var_row)
    sub = iota((16, LANES), 0)
    bias = small[cache_chunks + 2 : cache_chunks + 3, :] * LOG2E
    for head in range(heads):
        gain = bias[:, head : head + 1] - bias[:, heads + head : heads + head + 1]
        high, middle, low = three_parts(jnp.broadcast_to(gain, (16, LANES)))
        gains[head] = jnp.where(sub < 4, high, jnp.where(sub < 8, middle, low)).astype(BF16)


def arrange(cache, cache_values):
    for rows in blocks(cache.shape[1]):
        for cols in blocks(cache.shape[2]):
            cache_values[cols, rows] = cache[1, rows, cols].T


def turn_queries(piece, cosine, sine):
    turned = []
    for start in range(0, LANES, HEAD):
        x, y = piece[start : start + HALF, :], piece[start + HALF : start + HEAD, :]
        turned += [x * cosine - y * sine, y * cosine + x * sine]
    return (jnp.concatenate(turned, axis=0) * (0.125 * LOG2E)).astype(BF16)


def turn_keys(piece, cosine, sine):
    first = (iota(piece.shape, 1) & (HEAD - 1)) < HALF
    other = jnp.where(first, pltpu.roll(piece, LANES - HALF, 1), pltpu.roll(piece, HALF, 1))
    return (piece * cosine + other * sine).astype(BF16)


def project(
    first, second, weight, cosine, sine, key_cosine, key_sine, queries, keys, values, rows
):
    for chunk, block in enumerate((first, second)):
        rows[chunk * LANES : (chunk + 1) * LANES, :] = normed(block[...].astype(F32))
    for part in (1, 0, 2):
        product = dot(rows[...], weight[part])
        for chunk in range(2):
            for cols in blocks(product.shape[1]):
                piece = product[chunk * LANES : (chunk + 1) * LANES, cols]
                if part == 0:
                    queries[chunk, cols, :] = turn_queries(piece.T, cosine[chunk], sine[chunk])
                elif part == 1:
                    keys[chunk, :, cols] = turn_keys(piece, key_cosine[chunk], key_sine[chunk])
                else:
                    values[chunk, cols, :] = piece.T.astype(BF16)


def attend(queries, time_hot, var_hot, gains, keys, values, cache, cache_values, key_hot, emit):
    hot = key_hot[...].reshape(-1, LANES)
    ones = jnp.ones((16, hot.shape[0]), BF16)
    blank = jnp.zeros((HEAD, LANES), BF16)
    rest = jnp.zeros((LANES - HEAD - 16, LANES), BF16)
    chunks, width = len(queries), cache_values.shape[0]
    units = [(pair, chunk) for pair in range(width // LANES) for chunk in range(chunks)]
    left, right = [], []
    for cols in blocks(width):
        block = [cache[0, :, cols], keys[0, :, cols], keys[1, :, cols]]
        left.append(jnp.concatenate([jnp.concatenate(block, axis=0), hot], axis=1))
        block = [cache_values[cols, :], values[0, cols, :], values[1, cols, :]]
        right.append(jnp.concatenate([jnp.concatenate(block, axis=1), ones], axis=0))

    def features(pair, chunk):
        sides = []
        for side in range(2):
            head = 2 * pair + side
            query = queries[chunk][head * HEAD : (head + 1) * HEAD, :]
            both = [query, blank] if side == 0 else [blank, query]
            sides.append(
                jnp.concatenate(
                    both + [time_hot[chunk][...], var_hot[chunk][...] * gains[head], rest], axis=0
                )
            )
        return jnp.concatenate(sides, axis=1)

    scores, weights = {}, {}
    for step in range(len(units) + 2):
        if step < len(units):
            pair, chunk = units[step]
            scores[step] = dot(left[pair], features(pair, chunk))
        if 0 <= step - 1 < len(units):
            score = scores.pop(step - 1)
            top = jnp.max(score, axis=0, keepdims=True)
            weights[step - 1] = jnp.exp2(score - top).astype(BF16), top
        if 0 <= step - 2 < len(units):
            pair, chunk = units[step - 2]
            weight, top = weights.pop(step - 2)
            product = dot(right[pair], weight)
            for side in range(2):
                head, lanes = 2 * pair + side, slice(side * LANES, (side + 1) * LANES)
                total = product[LANES : LANES + 1, lanes]
                out = product[side * HEAD : (side + 1) * HEAD, lanes] * (1.0 / total)
                emit(chunk, head, out, top[:, lanes] + jnp.log2(total))


def attend_own(
    chunk, queries, time_hot, var_hot, gains, keys, values, cache, cache_values, key_hot, outputs, logs
):
    def emit(_, head, out, log):
        outputs[head * HEAD : (head + 1) * HEAD, :] = out
        logs[head : head + 1, :] = log

    rows = [[ref.at[chunk]] for ref in (queries, time_hot, var_hot)]
    attend(*rows, gains, keys, values, cache, cache_values, key_hot, emit)


def attend_far(
    chunk, by_owner, small, tokens, weight, gains, keys, values, cache, cache_values, key_hot, message, queries, logs
):
    width = cache_values.shape[0]
    time_hot, var_hot, cosine, sine = query_tables(*ids_of(small, chunk, by_owner))
    product = dot(normed(tokens[...].astype(F32)), weight[0])
    for cols in blocks(width):
        queries[cols, :] = turn_queries(product[:, cols].T, cosine, sine)
    logs[...] = jnp.zeros_like(logs)

    def emit(_, head, out, log):
        message[head * HEAD : (head + 1) * HEAD, :] = out.astype(BF16)
        logs[head : head + 1, :] = log

    attend(
        [queries], [time_hot], [var_hot], gains, keys, values, cache, cache_values, key_hot, emit
    )
    parts = list(three_parts(logs[...])) + [jnp.zeros((LOG_ROWS, LANES), F32)]
    message[width:, :] = jnp.concatenate(parts, axis=0).astype(BF16)


def join(own, own_log, *refs):
    *linked, weight, kept, sent = refs
    width = weight.shape[0]
    if linked:
        (message,) = linked
        stats = message[width:, :].astype(F32)
        far_log = stats[:8, :] + stats[8:16, :] + stats[16:24, :]
        share = 1.0 / (1.0 + jnp.exp2(far_log - own_log[...]))
    pieces = []
    for cols in blocks(width):
        joined = []
        for start in range(cols.start, cols.stop, HEAD):
            rows, head = slice(start, start + HEAD), start // HEAD
            part = own[rows, :]
            if linked:
                far = message[rows, :].astype(F32)
                part = far + (part - far) * share[head : head + 1, :]
            joined.append(part)
        pieces.append(jnp.concatenate(joined, axis=0).T.astype(BF16))
    product = dot(jnp.concatenate(pieces, axis=1), weight[...])
    kept[...] = product
    sent[...] = product.astype(BF16)


def feed(final, tokens, kept, received, gate_up, down, out):
    stream = (tokens[...].astype(F32) + kept[...] + received[...].astype(F32)).astype(BF16)
    stream = stream.astype(F32)
    rows = normed(stream)
    gate = dot(rows, gate_up[0])
    hidden = (gate / (1.0 + jnp.exp(-gate)) * dot(rows, gate_up[1])).astype(BF16)
    product = dot(hidden, down[...])
    out[...] = stream + product if final else product.astype(BF16)


def layer(
    with_partner,
    tokens,
    variate,
    time_ids,
    cache_var,
    cache_len,
    cache_kv,
    var_bias,
    w_qkv,
    w_out,
    w_gate_up,
    w_down,
):
    heads = var_bias.shape[1]
    width = cache_kv.shape[2]
    model = tokens.shape[1]
    cache_rows = cache_kv.shape[1]
    ways = lax.axis_size("tp")
    partner = lax.axis_size("group") // 2
    paired = ways == 2
    key_chunks = cache_rows // LANES + 2

    if with_partner:
        far_tokens = swap(tokens, "group", partner)
    if paired:
        other_tokens = swap(tokens, "tp", 1)
    small = jnp.concatenate(
        [
            (time_ids + HEAD * variate).astype(F32),
            cache_var.astype(F32),
            jnp.pad(var_bias.reshape(-1), (0, LANES - 2 * heads)),
        ]
    ).reshape(-1, LANES)
    if with_partner:
        far_small = swap(small, "group", partner)
    time_hot, var_hot, cosine, sine, key_cosine, key_sine, key_hot, gains = call(
        functools.partial(tables, paired, heads),
        [((2, HEAD, LANES), BF16), ((2, 16, LANES), BF16), ((2, HALF, LANES), F32), ((2, HALF, LANES), F32)]
        + [((2, LANES, LANES), F32)] * 2
        + [((key_chunks, LANES, LANES), BF16), ((heads, 16, LANES), BF16)],
        small, scalars=(cache_len,), flops=6_000_000_000,
    )
    (cache_values,) = call(arrange, [((width, cache_rows), BF16)], cache_kv)

    def all_rows(mine, other):
        if paired:
            return mine, other
        gathered = lax.all_gather(mine, "tp", axis=0, tiled=True)
        return gathered[:LANES], gathered[LANES:]

    own_rows = all_rows(tokens, other_tokens if paired else None)
    queries, keys, values = call(
        project,
        [((2, width, LANES), BF16), ((2, LANES, width), BF16), ((2, width, LANES), BF16)],
        *own_rows, w_qkv, cosine, sine, key_cosine, key_sine,
        flops=6 * 256 * model * width, scratch=[pltpu.VMEM((2 * LANES, model), BF16)],
    )
    key_side = (gains, keys, values, cache_kv, cache_values, key_hot)
    messages = []
    if with_partner:
        far_tokens, far_small, _ = lax.optimization_barrier((far_tokens, far_small, queries))
        far_rows = all_rows(far_tokens, swap(far_tokens, "tp", 1) if paired else None)

        def attended_for(index):
            (message,) = call(
                functools.partial(attend_far, index, paired), [((width + STAT_ROWS, LANES), BF16)],
                far_small, far_rows[index], w_qkv, *key_side, flops=8 * 128 * 768 * width,
                early=(w_gate_up, w_down, w_out) if index else (),
                scratch=[pltpu.VMEM((width, LANES), BF16), pltpu.VMEM((LOG_ROWS, LANES), F32)],
            )
            return message

        messages.append(attended_for(0))
        queries, _ = lax.optimization_barrier((queries, messages[0]))

    def attended(index):
        return call(
            functools.partial(attend_own, index), [((width, LANES), F32), ((LOG_ROWS, LANES), F32)],
            queries, time_hot, var_hot, *key_side, flops=8 * 128 * 768 * width,
        )

    own = [attended(0)]
    if not with_partner:
        own.append(attended(1))
    if with_partner:
        far_small, _ = lax.optimization_barrier((far_small, own[0]))
        messages.append(attended_for(1))
        queries, _ = lax.optimization_barrier((queries, messages[1]))
        own.append(attended(1))
        returned = [swap(message, "group", partner) for message in messages]
        returned[0], _ = lax.optimization_barrier((returned[0], messages[1]))
    kept, sent = [], []
    for index in range(2):
        extra = [returned[index]] if with_partner else []
        products = call(
            join, [((LANES, model), F32), ((LANES, model), BF16)], *own[index], *extra, w_out, flops=8_000_000_000,
        )
        kept.append(products[0])
        sent.append(products[1])

    def fed(index, final, part, received):
        (out,) = call(
            functools.partial(feed, final), [((LANES, model), F32 if final else BF16)],
            own_rows[index], part, received, w_gate_up, w_down,
            flops=6 * 128 * model * w_down.shape[0],
        )
        return out

    if paired:
        from_first = swap(sent[0], "tp", 1)
        if not with_partner:
            sent[1], from_first = lax.optimization_barrier((sent[1], from_first))
        from_second = swap(sent[1], "tp", 1)
        part = fed(1, False, kept[1], from_first)
        if not with_partner:
            part, from_second = lax.optimization_barrier((part, from_second))
        other = swap(part, "tp", 1)
        mine = fed(0, True, kept[0], from_second)
        return (mine + other.astype(F32)).astype(BF16)
    sums = [lax.psum(part, "tp") for part in sent]
    nothing = jnp.zeros((LANES, model), F32)
    parts = jnp.concatenate([fed(i, False, nothing, sums[i]) for i in range(2)])
    summed = lax.psum(parts, "tp")
    local = tokens.shape[0]
    start = lax.axis_index("tp") * local
    attended = lax.dynamic_slice_in_dim(jnp.concatenate(sums), start, local, 0)
    stream = (tokens.astype(F32) + attended.astype(F32)).astype(BF16).astype(F32)
    own_ffn = lax.dynamic_slice_in_dim(summed, start, local, 0).astype(F32)
    return (stream + own_ffn).astype(BF16)


def shards(tokens, variate, time_ids, cache_var, cache_len, linked, *rest):
    return lax.cond(
        linked[0] > 0,
        functools.partial(layer, True),
        functools.partial(layer, False),
        tokens, variate, time_ids, cache_var, cache_len, *rest,
    )


def solution(mesh):
    return jax.shard_map(
        shards,
        mesh=mesh,
        in_specs=(
            P(("group", "tp"), None),
            P("group"),
            P("group"),
            P("group"),
            P("group"),
            P("group"),
            P(None, "group", "tp"),
            P(None, "tp"),
            P(None, None, "tp"),
            P("tp", None),
            P(None, None, "tp"),
            P("tp", None),
        ),
        out_specs=P(("group", "tp"), None),
        check_vma=False,
    )
```

```python
import functools
import math

import jax
import jax.numpy as jnp
from jax import lax
from jax.experimental import pallas as pl
from jax.experimental.pallas import tpu as pltpu
from jax.sharding import PartitionSpec as P

LANES = 128
HEAD = 64
HALF = HEAD // 2
LOG_ROWS = 8
STAT_ROWS = 32
LOG2E = math.log2(math.e)
MASKED = -1e30
F32 = jnp.float32
BF16 = jnp.bfloat16

IN_VMEM = pl.BlockSpec(memory_space=pltpu.VMEM)
IN_SMEM = pl.BlockSpec(memory_space=pltpu.SMEM)


def call(body, outs, *operands, scalars=(), early=(), flops=0, scratch=()):
    if early:
        taken = len(scalars) + len(operands)
        inner = body

        def body(*refs):
            inner(*refs[:taken], *refs[taken + len(early) :])

        operands = (*operands, *early)
    shapes = [jax.ShapeDtypeStruct(shape, dtype) for shape, dtype in outs]
    moved = sum(x.size * x.dtype.itemsize for x in operands)
    return pl.pallas_call(
        body,
        out_shape=shapes,
        in_specs=[IN_SMEM] * len(scalars) + [IN_VMEM] * len(operands),
        out_specs=[IN_VMEM] * len(shapes),
        scratch_shapes=list(scratch),
        cost_estimate=pl.CostEstimate(flops=flops, bytes_accessed=moved, transcendentals=0),
        compiler_params=pltpu.CompilerParams(vmem_limit_bytes=16 << 20),
    )(*scalars, *operands)


def swap(block, axis, distance):
    count = lax.axis_size(axis)
    return lax.ppermute(block, axis, [(i, i ^ distance) for i in range(count)])


def normed(values):
    return (values * lax.rsqrt(jnp.mean(values * values, axis=-1, keepdims=True) + 1e-05)).astype(
        BF16
    )


def iota(shape, dim):
    return lax.broadcasted_iota(jnp.int32, shape, dim)


def dot(a, b):
    return jnp.dot(a, b, preferred_element_type=F32)


def three_parts(value):
    high = value.astype(BF16).astype(F32)
    middle = (value - high).astype(BF16).astype(F32)
    low = (value - high - middle).astype(BF16).astype(F32)
    return high, middle, low


def blocks(width):
    return [slice(start, start + LANES) for start in range(0, width, LANES)]


def place_of(chunk, by_owner):
    if not by_owner:
        return chunk
    return lax.axis_index("tp") if chunk == 0 else 1 - lax.axis_index("tp")


def ids_of(small, chunk, by_owner):
    ids = small[pl.ds(place_of(chunk, by_owner), 1), :].astype(jnp.int32)
    return ids & (HEAD - 1), ids >> 6


def query_tables(time_row, var_row):
    time_hot = jnp.where(iota((HEAD, LANES), 0) == time_row, 1.0, 0.0).astype(BF16)
    sub = iota((16, LANES), 0)
    var_hot = jnp.where((sub < 12) & ((sub & 3) == var_row), 1.0, 0.0).astype(BF16)
    angle = time_row.astype(F32) * jnp.exp(
        iota((HALF, LANES), 0).astype(F32) * (-math.log(10000.0) / HALF)
    )
    return time_hot, var_hot, jnp.cos(angle), jnp.sin(angle)


def key_table(hidden, var_row):
    sub = iota((LANES - HEAD, LANES), 0)
    same = jnp.where((sub < 12) & ((sub & 3) == var_row), 1.0, 0.0)
    return jnp.concatenate([jnp.where(hidden, MASKED, 0.0), same], axis=0).T.astype(BF16)


def tables(
    by_owner, heads, length, small, time_hot, var_hot, cosine, sine, key_cosine, key_sine, key_hot, gains
):
    cache_chunks = key_hot.shape[0] - 2
    for chunk in range(cache_chunks):
        slot = iota((HEAD, LANES), 1) + chunk * LANES
        cache_var = small[chunk + 2 : chunk + 3, :].astype(jnp.int32)
        key_hot[chunk] = key_table(slot >= length[0], cache_var)
    for chunk in range(2):
        time_row, var_row = ids_of(small, chunk, by_owner)
        time_hot[chunk], var_hot[chunk], cos, sin = query_tables(time_row, var_row)
        cosine[chunk], sine[chunk] = cos, sin
        key_cosine[chunk] = jnp.concatenate([cos] * 4, axis=0).T
        key_sine[chunk] = jnp.concatenate([-sin, sin, -sin, sin], axis=0).T
        key_hot[cache_chunks + chunk] = key_table(time_row > iota((HEAD, LANES), 0), var_row)
    sub = iota((16, LANES), 0)
    bias = small[cache_chunks + 2 : cache_chunks + 3, :]
    for head in range(heads):
        gain = bias[:, head : head + 1] - bias[:, heads + head : heads + head + 1]
        high, middle, low = three_parts(jnp.broadcast_to(gain, (16, LANES)))
        gains[head] = jnp.where(sub < 4, high, jnp.where(sub < 8, middle, low)).astype(BF16)


def arrange(cache, cache_values):
    for rows in blocks(cache.shape[1]):
        for cols in blocks(cache.shape[2]):
            cache_values[cols, rows] = cache[1, rows, cols].T


def turn_queries(piece, cosine, sine):
    turned = []
    for start in range(0, LANES, HEAD):
        x, y = piece[start : start + HALF, :], piece[start + HALF : start + HEAD, :]
        turned += [x * cosine - y * sine, y * cosine + x * sine]
    return (jnp.concatenate(turned, axis=0) * 0.125).astype(BF16)


def turn_keys(piece, cosine, sine):
    first = (iota(piece.shape, 1) & (HEAD - 1)) < HALF
    other = jnp.where(first, pltpu.roll(piece, LANES - HALF, 1), pltpu.roll(piece, HALF, 1))
    return (piece * cosine + other * sine).astype(BF16)


def project(
    first, second, weight, cosine, sine, key_cosine, key_sine, queries, keys, values, rows
):
    for chunk, block in enumerate((first, second)):
        rows[chunk * LANES : (chunk + 1) * LANES, :] = normed(block[...].astype(F32))
    for part in (1, 0, 2):
        product = dot(rows[...], weight[part])
        for chunk in range(2):
            for cols in blocks(product.shape[1]):
                piece = product[chunk * LANES : (chunk + 1) * LANES, cols]
                if part == 0:
                    queries[chunk, cols, :] = turn_queries(piece.T, cosine[chunk], sine[chunk])
                elif part == 1:
                    keys[chunk, :, cols] = turn_keys(piece, key_cosine[chunk], key_sine[chunk])
                else:
                    values[chunk, cols, :] = piece.T.astype(BF16)


def attend(queries, time_hot, var_hot, gains, keys, values, cache, cache_values, key_hot, emit):
    hot = key_hot[...].reshape(-1, LANES)
    ones = jnp.ones((16, hot.shape[0]), BF16)
    blank = jnp.zeros((HEAD, LANES), BF16)
    rest = jnp.zeros((LANES - HEAD - 16, LANES), BF16)
    chunks, width = len(queries), cache_values.shape[0]
    units = [(pair, chunk) for pair in range(width // LANES) for chunk in range(chunks)]
    left, right = [], []
    for cols in blocks(width):
        block = [cache[0, :, cols], keys[0, :, cols], keys[1, :, cols]]
        left.append(jnp.concatenate([jnp.concatenate(block, axis=0), hot], axis=1))
        block = [cache_values[cols, :], values[0, cols, :], values[1, cols, :]]
        right.append(jnp.concatenate([jnp.concatenate(block, axis=1), ones], axis=0))

    def features(pair, chunk):
        sides = []
        for side in range(2):
            head = 2 * pair + side
            query = queries[chunk][head * HEAD : (head + 1) * HEAD, :]
            both = [query, blank] if side == 0 else [blank, query]
            sides.append(
                jnp.concatenate(
                    both + [time_hot[chunk][...], var_hot[chunk][...] * gains[head], rest], axis=0
                )
            )
        return jnp.concatenate(sides, axis=1)

    scores, weights = {}, {}
    for step in range(len(units) + 2):
        if step < len(units):
            pair, chunk = units[step]
            scores[step] = dot(left[pair], features(pair, chunk))
        if 0 <= step - 1 < len(units):
            score = scores.pop(step - 1)
            top = jnp.max(score, axis=0, keepdims=True)
            weights[step - 1] = jnp.exp(score - top).astype(BF16), top
        if 0 <= step - 2 < len(units):
            pair, chunk = units[step - 2]
            weight, top = weights.pop(step - 2)
            product = dot(right[pair], weight)
            for side in range(2):
                head, lanes = 2 * pair + side, slice(side * LANES, (side + 1) * LANES)
                total = product[LANES : LANES + 1, lanes]
                out = product[side * HEAD : (side + 1) * HEAD, lanes] * (1.0 / total)
                emit(chunk, head, out, top[:, lanes] * LOG2E + jnp.log2(total))


def attend_own(
    chunk, queries, time_hot, var_hot, gains, keys, values, cache, cache_values, key_hot, outputs, logs
):
    def emit(_, head, out, log):
        outputs[head * HEAD : (head + 1) * HEAD, :] = out
        logs[head : head + 1, :] = log

    rows = [[ref.at[chunk]] for ref in (queries, time_hot, var_hot)]
    attend(*rows, gains, keys, values, cache, cache_values, key_hot, emit)


def attend_far(
    chunk, by_owner, small, tokens, weight, gains, keys, values, cache, cache_values, key_hot, message, queries, logs
):
    width = cache_values.shape[0]
    time_hot, var_hot, cosine, sine = query_tables(*ids_of(small, chunk, by_owner))
    product = dot(normed(tokens[...].astype(F32)), weight[0])
    for cols in blocks(width):
        queries[cols, :] = turn_queries(product[:, cols].T, cosine, sine)
    logs[...] = jnp.zeros_like(logs)

    def emit(_, head, out, log):
        message[head * HEAD : (head + 1) * HEAD, :] = out.astype(BF16)
        logs[head : head + 1, :] = log

    attend(
        [queries], [time_hot], [var_hot], gains, keys, values, cache, cache_values, key_hot, emit
    )
    parts = list(three_parts(logs[...])) + [jnp.zeros((LOG_ROWS, LANES), F32)]
    message[width:, :] = jnp.concatenate(parts, axis=0).astype(BF16)


def join(own, own_log, *refs):
    *linked, weight, kept, sent = refs
    width = weight.shape[0]
    if linked:
        (message,) = linked
        stats = message[width:, :].astype(F32)
        far_log = stats[:8, :] + stats[8:16, :] + stats[16:24, :]
        share = 1.0 / (1.0 + jnp.exp2(far_log - own_log[...]))
    pieces = []
    for cols in blocks(width):
        joined = []
        for start in range(cols.start, cols.stop, HEAD):
            rows, head = slice(start, start + HEAD), start // HEAD
            part = own[rows, :]
            if linked:
                far = message[rows, :].astype(F32)
                part = far + (part - far) * share[head : head + 1, :]
            joined.append(part)
        pieces.append(jnp.concatenate(joined, axis=0).T.astype(BF16))
    product = dot(jnp.concatenate(pieces, axis=1), weight[...])
    kept[...] = product
    sent[...] = product.astype(BF16)


def feed(final, tokens, kept, received, gate_up, down, out):
    stream = (tokens[...].astype(F32) + kept[...] + received[...].astype(F32)).astype(BF16)
    stream = stream.astype(F32)
    rows = normed(stream)
    gate = dot(rows, gate_up[0])
    hidden = (gate / (1.0 + jnp.exp(-gate)) * dot(rows, gate_up[1])).astype(BF16)
    product = dot(hidden, down[...])
    out[...] = stream + product if final else product.astype(BF16)


def layer(
    with_partner,
    tokens,
    variate,
    time_ids,
    cache_var,
    cache_len,
    cache_kv,
    var_bias,
    w_qkv,
    w_out,
    w_gate_up,
    w_down,
):
    heads = var_bias.shape[1]
    width = cache_kv.shape[2]
    model = tokens.shape[1]
    cache_rows = cache_kv.shape[1]
    ways = lax.axis_size("tp")
    partner = lax.axis_size("group") // 2
    paired = ways == 2
    key_chunks = cache_rows // LANES + 2

    if with_partner:
        far_tokens = swap(tokens, "group", partner)
    if paired:
        other_tokens = swap(tokens, "tp", 1)
    small = jnp.concatenate(
        [
            (time_ids + HEAD * variate).astype(F32),
            cache_var.astype(F32),
            jnp.pad(var_bias.reshape(-1), (0, LANES - 2 * heads)),
        ]
    ).reshape(-1, LANES)
    if with_partner:
        far_small = swap(small, "group", partner)
    time_hot, var_hot, cosine, sine, key_cosine, key_sine, key_hot, gains = call(
        functools.partial(tables, paired, heads),
        [((2, HEAD, LANES), BF16), ((2, 16, LANES), BF16), ((2, HALF, LANES), F32), ((2, HALF, LANES), F32)]
        + [((2, LANES, LANES), F32)] * 2
        + [((key_chunks, LANES, LANES), BF16), ((heads, 16, LANES), BF16)],
        small, scalars=(cache_len,), flops=6_000_000_000,
    )
    (cache_values,) = call(arrange, [((width, cache_rows), BF16)], cache_kv)

    def all_rows(mine, other):
        if paired:
            return mine, other
        gathered = lax.all_gather(mine, "tp", axis=0, tiled=True)
        return gathered[:LANES], gathered[LANES:]

    own_rows = all_rows(tokens, other_tokens if paired else None)
    queries, keys, values = call(
        project,
        [((2, width, LANES), BF16), ((2, LANES, width), BF16), ((2, width, LANES), BF16)],
        *own_rows, w_qkv, cosine, sine, key_cosine, key_sine,
        flops=6 * 256 * model * width, scratch=[pltpu.VMEM((2 * LANES, model), BF16)],
    )
    key_side = (gains, keys, values, cache_kv, cache_values, key_hot)
    messages = []
    if with_partner:
        far_tokens, far_small, _ = lax.optimization_barrier((far_tokens, far_small, queries))
        far_rows = all_rows(far_tokens, swap(far_tokens, "tp", 1) if paired else None)

        def attended_for(index):
            (message,) = call(
                functools.partial(attend_far, index, paired), [((width + STAT_ROWS, LANES), BF16)],
                far_small, far_rows[index], w_qkv, *key_side, flops=8 * 128 * 768 * width,
                early=(w_gate_up, w_down, w_out) if index else (),
                scratch=[pltpu.VMEM((width, LANES), BF16), pltpu.VMEM((LOG_ROWS, LANES), F32)],
            )
            return message

        messages.append(attended_for(0))
        queries, _ = lax.optimization_barrier((queries, messages[0]))

    def attended(index):
        return call(
            functools.partial(attend_own, index), [((width, LANES), F32), ((LOG_ROWS, LANES), F32)],
            queries, time_hot, var_hot, *key_side, flops=8 * 128 * 768 * width,
        )

    own = [attended(0)]
    if not with_partner:
        own.append(attended(1))
    if with_partner:
        far_small, _ = lax.optimization_barrier((far_small, own[0]))
        messages.append(attended_for(1))
        queries, _ = lax.optimization_barrier((queries, messages[1]))
        own.append(attended(1))
        returned = [swap(message, "group", partner) for message in messages]
        returned[0], _ = lax.optimization_barrier((returned[0], messages[1]))
    kept, sent = [], []
    for index in range(2):
        extra = [returned[index]] if with_partner else []
        products = call(
            join, [((LANES, model), F32), ((LANES, model), BF16)], *own[index], *extra, w_out, flops=8_000_000_000,
        )
        kept.append(products[0])
        sent.append(products[1])

    def fed(index, final, part, received):
        (out,) = call(
            functools.partial(feed, final), [((LANES, model), F32 if final else BF16)],
            own_rows[index], part, received, w_gate_up, w_down,
            flops=6 * 128 * model * w_down.shape[0],
        )
        return out

    if paired:
        from_first = swap(sent[0], "tp", 1)
        if not with_partner:
            sent[1], from_first = lax.optimization_barrier((sent[1], from_first))
        from_second = swap(sent[1], "tp", 1)
        part = fed(1, False, kept[1], from_first)
        if not with_partner:
            part, from_second = lax.optimization_barrier((part, from_second))
        other = swap(part, "tp", 1)
        mine = fed(0, True, kept[0], from_second)
        return (mine + other.astype(F32)).astype(BF16)
    sums = [lax.psum(part, "tp") for part in sent]
    nothing = jnp.zeros((LANES, model), F32)
    parts = jnp.concatenate([fed(i, False, nothing, sums[i]) for i in range(2)])
    summed = lax.psum(parts, "tp")
    local = tokens.shape[0]
    start = lax.axis_index("tp") * local
    attended = lax.dynamic_slice_in_dim(jnp.concatenate(sums), start, local, 0)
    stream = (tokens.astype(F32) + attended.astype(F32)).astype(BF16).astype(F32)
    own_ffn = lax.dynamic_slice_in_dim(summed, start, local, 0).astype(F32)
    return (stream + own_ffn).astype(BF16)


def shards(tokens, variate, time_ids, cache_var, cache_len, linked, *rest):
    return lax.cond(
        linked[0] > 0,
        functools.partial(layer, True),
        functools.partial(layer, False),
        tokens, variate, time_ids, cache_var, cache_len, *rest,
    )


def solution(mesh):
    return jax.shard_map(
        shards,
        mesh=mesh,
        in_specs=(
            P(("group", "tp"), None),
            P("group"),
            P("group"),
            P("group"),
            P("group"),
            P("group"),
            P(None, "group", "tp"),
            P(None, "tp"),
            P(None, None, "tp"),
            P("tp", None),
            P(None, None, "tp"),
            P("tp", None),
        ),
        out_specs=P(("group", "tp"), None),
        check_vma=False,
    )
```

```python
import functools
import math

import jax
import jax.numpy as jnp
from jax import lax
from jax.experimental import pallas as pl
from jax.experimental.pallas import tpu as pltpu
from jax.sharding import PartitionSpec as P

LANES = 128
HEAD = 64
HALF = HEAD // 2
LOG_ROWS = 8
STAT_ROWS = 32
LOG2E = math.log2(math.e)
MASKED = -1e30
F32 = jnp.float32
BF16 = jnp.bfloat16

IN_VMEM = pl.BlockSpec(memory_space=pltpu.VMEM)
IN_SMEM = pl.BlockSpec(memory_space=pltpu.SMEM)


def call(body, outs, *operands, scalars=(), early=(), flops=0, scratch=()):
    if early:
        taken = len(scalars) + len(operands)
        inner = body

        def body(*refs):
            inner(*refs[:taken], *refs[taken + len(early) :])

        operands = (*operands, *early)
    shapes = [jax.ShapeDtypeStruct(shape, dtype) for shape, dtype in outs]
    moved = sum(x.size * x.dtype.itemsize for x in operands)
    return pl.pallas_call(
        body,
        out_shape=shapes,
        in_specs=[IN_SMEM] * len(scalars) + [IN_VMEM] * len(operands),
        out_specs=[IN_VMEM] * len(shapes),
        scratch_shapes=list(scratch),
        cost_estimate=pl.CostEstimate(flops=flops, bytes_accessed=moved, transcendentals=0),
        compiler_params=pltpu.CompilerParams(vmem_limit_bytes=16 << 20),
    )(*scalars, *operands)


def swap(block, axis, distance):
    count = lax.axis_size(axis)
    return lax.ppermute(block, axis, [(i, i ^ distance) for i in range(count)])


def normed(values):
    return (values * lax.rsqrt(jnp.mean(values * values, axis=-1, keepdims=True) + 1e-05)).astype(
        BF16
    )


def iota(shape, dim):
    return lax.broadcasted_iota(jnp.int32, shape, dim)


def dot(a, b):
    return jnp.dot(a, b, preferred_element_type=F32)


def three_parts(value):
    high = value.astype(BF16).astype(F32)
    middle = (value - high).astype(BF16).astype(F32)
    low = (value - high - middle).astype(BF16).astype(F32)
    return high, middle, low


def blocks(width):
    return [slice(start, start + LANES) for start in range(0, width, LANES)]


def place_of(chunk, by_owner):
    if not by_owner:
        return chunk
    return lax.axis_index("tp") if chunk == 0 else 1 - lax.axis_index("tp")


def ids_of(small, chunk, by_owner):
    ids = small[pl.ds(place_of(chunk, by_owner), 1), :].astype(jnp.int32)
    return ids & (HEAD - 1), ids >> 6


def query_tables(time_row, var_row):
    time_hot = jnp.where(iota((HEAD, LANES), 0) == time_row, 1.0, 0.0).astype(BF16)
    sub = iota((16, LANES), 0)
    var_hot = jnp.where((sub < 12) & ((sub & 3) == var_row), 1.0, 0.0).astype(BF16)
    angle = time_row.astype(F32) * jnp.exp(
        iota((HALF, LANES), 0).astype(F32) * (-math.log(10000.0) / HALF)
    )
    return time_hot, var_hot, jnp.cos(angle), jnp.sin(angle)


def key_table(hidden, var_row):
    sub = iota((LANES - HEAD, LANES), 0)
    same = jnp.where((sub < 12) & ((sub & 3) == var_row), 1.0, 0.0)
    return jnp.concatenate([jnp.where(hidden, MASKED, 0.0), same], axis=0).T.astype(BF16)


def tables(
    by_owner, heads, length, small, time_hot, var_hot, cosine, sine, key_cosine, key_sine, key_hot, gains
):
    cache_chunks = key_hot.shape[0] - 2
    for chunk in range(cache_chunks):
        slot = iota((HEAD, LANES), 1) + chunk * LANES
        cache_var = small[chunk + 2 : chunk + 3, :].astype(jnp.int32)
        key_hot[chunk] = key_table(slot >= length[0], cache_var)
    for chunk in range(2):
        time_row, var_row = ids_of(small, chunk, by_owner)
        time_hot[chunk], var_hot[chunk], cos, sin = query_tables(time_row, var_row)
        cosine[chunk], sine[chunk] = cos, sin
        key_cosine[chunk] = jnp.concatenate([cos] * 4, axis=0).T
        key_sine[chunk] = jnp.concatenate([-sin, sin, -sin, sin], axis=0).T
        key_hot[cache_chunks + chunk] = key_table(time_row > iota((HEAD, LANES), 0), var_row)
    sub = iota((16, LANES), 0)
    bias = small[cache_chunks + 2 : cache_chunks + 3, :]
    for head in range(heads):
        gain = bias[:, head : head + 1] - bias[:, heads + head : heads + head + 1]
        high, middle, low = three_parts(jnp.broadcast_to(gain, (16, LANES)))
        gains[head] = jnp.where(sub < 4, high, jnp.where(sub < 8, middle, low)).astype(BF16)


def largest_norm(rows, out):
    width = rows.shape[1]
    head = iota((width, LANES), 0) // HEAD == iota((width, LANES), 1)
    squares = rows.astype(F32) * rows.astype(F32)
    sums = dot(squares.astype(BF16), jnp.where(head, 1.0, 0.0).astype(BF16))
    largest = jnp.max(jnp.max(sums, axis=0, keepdims=True), axis=1, keepdims=True)
    out[...] = jnp.broadcast_to(largest, out.shape)


def arrange(cache, cache_values, cache_norm):
    largest_norm(cache[0], cache_norm)
    for rows in blocks(cache.shape[1]):
        for cols in blocks(cache.shape[2]):
            cache_values[cols, rows] = cache[1, rows, cols].T


def turn_queries(piece, cosine, sine):
    turned = []
    for start in range(0, LANES, HEAD):
        x, y = piece[start : start + HALF, :], piece[start + HALF : start + HEAD, :]
        turned += [x * cosine - y * sine, y * cosine + x * sine]
    return (jnp.concatenate(turned, axis=0) * 0.125).astype(BF16)


def turn_keys(piece, cosine, sine):
    first = (iota(piece.shape, 1) & (HEAD - 1)) < HALF
    other = jnp.where(first, pltpu.roll(piece, LANES - HALF, 1), pltpu.roll(piece, HALF, 1))
    return (piece * cosine + other * sine).astype(BF16)


def project(
    first, second, weight, cosine, sine, key_cosine, key_sine, queries, keys, values, key_norm, rows
):
    for chunk, block in enumerate((first, second)):
        rows[chunk * LANES : (chunk + 1) * LANES, :] = normed(block[...].astype(F32))
    for part in (1, 0, 2):
        product = dot(rows[...], weight[part])
        for chunk in range(2):
            for cols in blocks(product.shape[1]):
                piece = product[chunk * LANES : (chunk + 1) * LANES, cols]
                if part == 0:
                    queries[chunk, cols, :] = turn_queries(piece.T, cosine[chunk], sine[chunk])
                elif part == 1:
                    keys[chunk, :, cols] = turn_keys(piece, key_cosine[chunk], key_sine[chunk])
                else:
                    values[chunk, cols, :] = piece.T.astype(BF16)
    largest_norm(keys[...].reshape(2 * LANES, -1), key_norm)


def attend(queries, time_hot, var_hot, gains, keys, values, cache, cache_values, key_hot, key_norm, cache_norm, emit):
    longest = 0.0
    for query in queries:
        squares = query[...].astype(F32) * query[...].astype(F32)
        for start in range(0, squares.shape[0], HEAD):
            longest = jnp.maximum(longest, jnp.sum(squares[start : start + HEAD], axis=0, keepdims=True))
    small = jnp.max(longest) * jnp.max(jnp.maximum(key_norm[...], cache_norm[...])) < 50.0**2
    sources = (
        queries, time_hot, var_hot, gains, keys, values, cache, cache_values, key_hot, emit
    )

    @pl.when(small)
    def _():
        attend_units(False, *sources)

    @pl.when(jnp.logical_not(small))
    def _():
        attend_units(True, *sources)


def attend_units(
    shifted, queries, time_hot, var_hot, gains, keys, values, cache, cache_values, key_hot, emit
):
    hot = key_hot[...].reshape(-1, LANES)
    ones = jnp.ones((16, hot.shape[0]), BF16)
    blank = jnp.zeros((HEAD, LANES), BF16)
    rest = jnp.zeros((LANES - HEAD - 16, LANES), BF16)
    chunks, width = len(queries), cache_values.shape[0]
    units = [(pair, chunk) for pair in range(width // LANES) for chunk in range(chunks)]
    left, right = [], []
    for cols in blocks(width):
        block = [cache[0, :, cols], keys[0, :, cols], keys[1, :, cols]]
        left.append(jnp.concatenate([jnp.concatenate(block, axis=0), hot], axis=1))
        block = [cache_values[cols, :], values[0, cols, :], values[1, cols, :]]
        right.append(jnp.concatenate([jnp.concatenate(block, axis=1), ones], axis=0))

    def features(pair, chunk):
        sides = []
        for side in range(2):
            head = 2 * pair + side
            query = queries[chunk][head * HEAD : (head + 1) * HEAD, :]
            both = [query, blank] if side == 0 else [blank, query]
            sides.append(
                jnp.concatenate(
                    both + [time_hot[chunk][...], var_hot[chunk][...] * gains[head], rest], axis=0
                )
            )
        return jnp.concatenate(sides, axis=1)

    scores, weights = {}, {}
    for step in range(len(units) + 2):
        if step < len(units):
            pair, chunk = units[step]
            scores[step] = dot(left[pair], features(pair, chunk))
        if 0 <= step - 1 < len(units):
            score = scores.pop(step - 1)
            top = jnp.max(score, axis=0, keepdims=True) if shifted else 0.0
            weights[step - 1] = jnp.exp(score - top if shifted else score).astype(BF16), top
        if 0 <= step - 2 < len(units):
            pair, chunk = units[step - 2]
            weight, top = weights.pop(step - 2)
            product = dot(right[pair], weight)
            for side in range(2):
                head, lanes = 2 * pair + side, slice(side * LANES, (side + 1) * LANES)
                total = product[LANES : LANES + 1, lanes]
                out = product[side * HEAD : (side + 1) * HEAD, lanes] * (1.0 / total)
                log = jnp.log2(total)
                emit(chunk, head, out, log + top[:, lanes] * LOG2E if shifted else log)


def attend_own(
    chunk, queries, time_hot, var_hot, gains, keys, values, cache, cache_values, key_hot, key_norm, cache_norm, outputs, logs
):
    def emit(_, head, out, log):
        outputs[head * HEAD : (head + 1) * HEAD, :] = out
        logs[head : head + 1, :] = log

    rows = [[ref.at[chunk]] for ref in (queries, time_hot, var_hot)]
    attend(*rows, gains, keys, values, cache, cache_values, key_hot, key_norm, cache_norm, emit)


def attend_far(
    chunk, by_owner, small, tokens, weight, gains, keys, values, cache, cache_values, key_hot, key_norm, cache_norm, message, queries, logs
):
    width = cache_values.shape[0]
    time_hot, var_hot, cosine, sine = query_tables(*ids_of(small, chunk, by_owner))
    product = dot(normed(tokens[...].astype(F32)), weight[0])
    for cols in blocks(width):
        queries[cols, :] = turn_queries(product[:, cols].T, cosine, sine)
    logs[...] = jnp.zeros_like(logs)

    def emit(_, head, out, log):
        message[head * HEAD : (head + 1) * HEAD, :] = out.astype(BF16)
        logs[head : head + 1, :] = log

    attend(
        [queries], [time_hot], [var_hot], gains, keys, values, cache, cache_values, key_hot, key_norm, cache_norm, emit
    )
    parts = list(three_parts(logs[...])) + [jnp.zeros((LOG_ROWS, LANES), F32)]
    message[width:, :] = jnp.concatenate(parts, axis=0).astype(BF16)


def join(own, own_log, *refs):
    *linked, weight, kept, sent = refs
    width = weight.shape[0]
    if linked:
        (message,) = linked
        stats = message[width:, :].astype(F32)
        far_log = stats[:8, :] + stats[8:16, :] + stats[16:24, :]
        share = 1.0 / (1.0 + jnp.exp2(far_log - own_log[...]))
    pieces = []
    for cols in blocks(width):
        joined = []
        for start in range(cols.start, cols.stop, HEAD):
            rows, head = slice(start, start + HEAD), start // HEAD
            part = own[rows, :]
            if linked:
                far = message[rows, :].astype(F32)
                part = far + (part - far) * share[head : head + 1, :]
            joined.append(part)
        pieces.append(jnp.concatenate(joined, axis=0).T.astype(BF16))
    product = dot(jnp.concatenate(pieces, axis=1), weight[...])
    kept[...] = product
    sent[...] = product.astype(BF16)


def feed(final, tokens, kept, received, gate_up, down, out):
    stream = (tokens[...].astype(F32) + kept[...] + received[...].astype(F32)).astype(BF16)
    stream = stream.astype(F32)
    rows = normed(stream)
    gate = dot(rows, gate_up[0])
    hidden = (gate / (1.0 + jnp.exp(-gate)) * dot(rows, gate_up[1])).astype(BF16)
    product = dot(hidden, down[...])
    out[...] = stream + product if final else product.astype(BF16)


def layer(
    with_partner,
    tokens,
    variate,
    time_ids,
    cache_var,
    cache_len,
    cache_kv,
    var_bias,
    w_qkv,
    w_out,
    w_gate_up,
    w_down,
):
    heads = var_bias.shape[1]
    width = cache_kv.shape[2]
    model = tokens.shape[1]
    cache_rows = cache_kv.shape[1]
    ways = lax.axis_size("tp")
    partner = lax.axis_size("group") // 2
    paired = ways == 2
    key_chunks = cache_rows // LANES + 2

    if with_partner:
        far_tokens = swap(tokens, "group", partner)
    if paired:
        other_tokens = swap(tokens, "tp", 1)
    small = jnp.concatenate(
        [
            (time_ids + HEAD * variate).astype(F32),
            cache_var.astype(F32),
            jnp.pad(var_bias.reshape(-1), (0, LANES - 2 * heads)),
        ]
    ).reshape(-1, LANES)
    if with_partner:
        far_small = swap(small, "group", partner)
    time_hot, var_hot, cosine, sine, key_cosine, key_sine, key_hot, gains = call(
        functools.partial(tables, paired, heads),
        [((2, HEAD, LANES), BF16), ((2, 16, LANES), BF16), ((2, HALF, LANES), F32), ((2, HALF, LANES), F32)]
        + [((2, LANES, LANES), F32)] * 2
        + [((key_chunks, LANES, LANES), BF16), ((heads, 16, LANES), BF16)],
        small, scalars=(cache_len,), flops=6_000_000_000,
    )
    cache_values, cache_norm = call(
        arrange, [((width, cache_rows), BF16), ((8, LANES), F32)], cache_kv
    )

    def all_rows(mine, other):
        if paired:
            return mine, other
        gathered = lax.all_gather(mine, "tp", axis=0, tiled=True)
        return gathered[:LANES], gathered[LANES:]

    own_rows = all_rows(tokens, other_tokens if paired else None)
    queries, keys, values, key_norm = call(
        project,
        [((2, width, LANES), BF16), ((2, LANES, width), BF16), ((2, width, LANES), BF16), ((8, LANES), F32)],
        *own_rows, w_qkv, cosine, sine, key_cosine, key_sine,
        flops=6 * 256 * model * width, scratch=[pltpu.VMEM((2 * LANES, model), BF16)],
    )
    key_side = (gains, keys, values, cache_kv, cache_values, key_hot, key_norm, cache_norm)
    messages = []
    if with_partner:
        far_tokens, far_small, _ = lax.optimization_barrier((far_tokens, far_small, queries))
        far_rows = all_rows(far_tokens, swap(far_tokens, "tp", 1) if paired else None)

        def attended_for(index):
            (message,) = call(
                functools.partial(attend_far, index, paired), [((width + STAT_ROWS, LANES), BF16)],
                far_small, far_rows[index], w_qkv, *key_side, flops=8 * 128 * 768 * width,
                early=(w_gate_up, w_down, w_out) if index else (),
                scratch=[pltpu.VMEM((width, LANES), BF16), pltpu.VMEM((LOG_ROWS, LANES), F32)],
            )
            return message

        messages.append(attended_for(0))
        queries, _ = lax.optimization_barrier((queries, messages[0]))

    def attended(index):
        return call(
            functools.partial(attend_own, index), [((width, LANES), F32), ((LOG_ROWS, LANES), F32)],
            queries, time_hot, var_hot, *key_side, flops=8 * 128 * 768 * width,
        )

    own = [attended(0)]
    if not with_partner:
        own.append(attended(1))
    if with_partner:
        far_small, _ = lax.optimization_barrier((far_small, own[0]))
        messages.append(attended_for(1))
        queries, _ = lax.optimization_barrier((queries, messages[1]))
        own.append(attended(1))
        returned = [swap(message, "group", partner) for message in messages]
        returned[0], _ = lax.optimization_barrier((returned[0], messages[1]))
    kept, sent = [], []
    for index in range(2):
        extra = [returned[index]] if with_partner else []
        products = call(
            join, [((LANES, model), F32), ((LANES, model), BF16)], *own[index], *extra, w_out, flops=8_000_000_000,
        )
        kept.append(products[0])
        sent.append(products[1])

    def fed(index, final, part, received):
        (out,) = call(
            functools.partial(feed, final), [((LANES, model), F32 if final else BF16)],
            own_rows[index], part, received, w_gate_up, w_down,
            flops=6 * 128 * model * w_down.shape[0],
        )
        return out

    if paired:
        from_first = swap(sent[0], "tp", 1)
        if not with_partner:
            sent[1], from_first = lax.optimization_barrier((sent[1], from_first))
        from_second = swap(sent[1], "tp", 1)
        part = fed(1, False, kept[1], from_first)
        if not with_partner:
            part, from_second = lax.optimization_barrier((part, from_second))
        other = swap(part, "tp", 1)
        mine = fed(0, True, kept[0], from_second)
        return (mine + other.astype(F32)).astype(BF16)
    sums = [lax.psum(part, "tp") for part in sent]
    nothing = jnp.zeros((LANES, model), F32)
    parts = jnp.concatenate([fed(i, False, nothing, sums[i]) for i in range(2)])
    summed = lax.psum(parts, "tp")
    local = tokens.shape[0]
    start = lax.axis_index("tp") * local
    attended = lax.dynamic_slice_in_dim(jnp.concatenate(sums), start, local, 0)
    stream = (tokens.astype(F32) + attended.astype(F32)).astype(BF16).astype(F32)
    own_ffn = lax.dynamic_slice_in_dim(summed, start, local, 0).astype(F32)
    return (stream + own_ffn).astype(BF16)


def shards(tokens, variate, time_ids, cache_var, cache_len, linked, *rest):
    return lax.cond(
        linked[0] > 0,
        functools.partial(layer, True),
        functools.partial(layer, False),
        tokens, variate, time_ids, cache_var, cache_len, *rest,
    )


def solution(mesh):
    return jax.shard_map(
        shards,
        mesh=mesh,
        in_specs=(
            P(("group", "tp"), None),
            P("group"),
            P("group"),
            P("group"),
            P("group"),
            P("group"),
            P(None, "group", "tp"),
            P(None, "tp"),
            P(None, None, "tp"),
            P("tp", None),
            P(None, None, "tp"),
            P("tp", None),
        ),
        out_specs=P(("group", "tp"), None),
        check_vma=False,
    )
```
